32 devices in a mesh: section: 2 (over x), dp: 4 (over z), fsdp: 4 (over y, core).
Axes of the slice: x: 2, y: 2, z: 4, core: 2. Of those that a mesh axis runs over, the one named last changes fastest.
Arguments:
- tokens: bfloat16 [2, 2048, 768], P(None, ('dp', 'fsdp')), may hold values from -6 to 6
- cotangent: bfloat16 [2, 2048, 768], P(None, ('dp', 'fsdp')), may hold values from -6 to 6
- lengths: int32 [2, 16], P(None, ('dp', 'fsdp')), may hold values from 1 to 128, 1280 in all within a row
- norm_gain: bfloat16 [2, 768], P('section', 'fsdp'), may hold values from 0.099609375 to 1.8984375
- in_weight: bfloat16 [2, 768, 3328], P('section', 'fsdp'), may hold values from -0.21875 to 0.21875
- dt_weight: bfloat16 [2, 768, 24], P('section', 'fsdp'), may hold values from -0.21875 to 0.21875
- conv_weight: bfloat16 [2, 4, 1792], P('section', None, 'fsdp'), may hold values from -3 to 3
- conv_bias: bfloat16 [2, 1792], P('section', 'fsdp'), may hold values from -3 to 3
- dt_bias: bfloat16 [2, 24], P('section', 'fsdp'), may hold values from -4 to -1
- a_log: bfloat16 [2, 24], P('section', 'fsdp'), may hold values from -3 to 1
- skip: bfloat16 [2, 24], P('section', 'fsdp'), may hold values from 0.5 to 1.5
- gated_gain: bfloat16 [2, 1536], P('section', 'fsdp'), may hold values from 0.099609375 to 1.8984375
- out_weight: bfloat16 [2, 1536, 768], P('section', 'fsdp'), may hold values from -0.15625 to 0.15625
Outputs:
- section_outputs: bfloat16 [2, 2, 2048, 768], P('section', None, ('dp', 'fsdp'))
- section_input_grads: float32 [2, 2, 2048, 768], P('section', None, ('dp', 'fsdp'))
- norm_gain_grad: float32 [2, 768], P('section', 'fsdp')
- in_weight_grad: float32 [2, 768, 3328], P('section', 'fsdp')
- dt_weight_grad: float32 [2, 768, 24], P('section', 'fsdp')
- conv_weight_grad: float32 [2, 4, 1792], P('section', None, 'fsdp')
- conv_bias_grad: float32 [2, 1792], P('section', 'fsdp')
- dt_bias_grad: float32 [2, 24], P('section', 'fsdp')
- a_log_grad: float32 [2, 24], P('section', 'fsdp')
- skip_grad: float32 [2, 24], P('section', 'fsdp')
- gated_gain_grad: float32 [2, 1536], P('section', 'fsdp')
- out_weight_grad: float32 [2, 1536, 768], P('section', 'fsdp')
The draws below stay inside these ranges and needn't reach their ends.
Inputs may be any that keep to these rules, and one draw needn't show every extreme that they name: In each micro-batch the lengths sum to 1280 and one of them is 128.
All inputs are finite; a program needn't handle non-finite values. No bound on the sum of `lengths` on one device may be relied on, other than what follows from the above.
Results may differ from the reference program's by a relative error of at most 0.02.
Values may be sent and summed in bfloat16 or wider, within the bound.
No kernel may reach another device: no remote copies, remote signals or barrier semaphores. Data moves between devices by JAX's collectives and lax.ppermute only.
A program may use at most 256 MiB of HBM per device.

```python
import math
import jax
import jax.numpy as jnp
import numpy as np
from jax import lax

D = 768
INNER = 1536
HEADS = 24
STATE = 128
HEAD_DIM = 64
CONV = 4
SPAN = 256
MB = 2
SEQ = 128
XBC = 1792
PROJ = 3328
TOKENS = 2048
TOTAL_LEN = 1280
N_SECTION = 2
N_DP = 4
N_FSDP = 4


def block_scale(key, dims, cuts, smallest, largest):
    factor_of = 1.0
    for position, shards_of in cuts:
        steps = jax.random.uniform(jax.random.fold_in(jax.random.fold_in(key, 6), position), (shards_of,), jnp.float32, smallest / len(cuts), largest / len(cuts))
        factor_of = factor_of * jnp.repeat(jnp.exp(steps), dims[position] // shards_of).reshape((-1,) + (1,) * (len(dims) - 1 - position))
    return factor_of


def length_profile(count, total, bound, slope):
    portions = [(1 << 20) // math.isqrt(standing ** slope) + 1 for standing in range(2, count + 1)]
    surplus, holding = total - bound - (count - 1), [1] * (count - 1)
    while surplus > 0:
        candidates = [i for i in range(count - 1) if holding[i] < bound]
        pool, remaining = sum([portions[i] for i in candidates]), surplus
        for i in candidates:
            extra = min(bound - holding[i], max(1, remaining * portions[i] // pool), surplus)
            holding[i] = holding[i] + extra
            surplus = surplus - extra
    return np.array([bound] + holding)


def uneven_parts(rng, amount, total, bound, slope):
    if amount == 2:
        one = jax.random.randint(rng, (), max(1, total - bound), min(bound, total - 1) + 1)
        return jnp.stack([one, total - one])
    sizes = jnp.asarray(length_profile(amount, total, bound, slope), jnp.int32)
    couples = (amount - 1) // 2
    giver, taker = sizes[1:1 + 2 * couples:2], sizes[2:2 + 2 * couples:2]
    margin = jnp.minimum(giver - 1, bound - taker)
    shifted = jax.random.randint(jax.random.fold_in(rng, 1), (couples,), 0, 1 << 20) % (margin + 1)
    sizes = sizes.at[1:1 + 2 * couples:2].set(giver - shifted).at[2:2 + 2 * couples:2].set(taker + shifted)
    return sizes[jax.random.permutation(jax.random.fold_in(rng, 2), amount)]


def noise(rng, extent, deviation, reach, shards=(), kind=jnp.bfloat16):
    factor_of = block_scale(rng, extent, shards, -0.22, 0.18) if shards else 1.0
    values = jax.random.normal(rng, extent, jnp.float32) * deviation * factor_of
    return jnp.minimum(jnp.maximum(values, -reach), reach).astype(kind)


def setup_inputs(seed: int = 0) -> dict:
    splits = jax.random.split(jax.random.key(seed), 14)
    return {
        "tokens": noise(splits[0], (MB, TOKENS, D), 1.0, 6.0, ((1, 16),)),
        "cotangent": noise(splits[1], (MB, TOKENS, D), 1.0, 6.0, ((1, 16),)),
        "lengths": jax.vmap(lambda own: uneven_parts(own, N_DP * N_FSDP, TOTAL_LEN, SEQ, 2))(jax.random.split(splits[2], MB)).reshape((MB, N_DP * N_FSDP)).astype(jnp.int32),
        "norm_gain": jnp.clip(1.0 + 0.18 * jax.random.normal(splits[3], (N_SECTION, D), jnp.float32), 0.099609375, 1.8984375).astype(jnp.bfloat16),
        "in_weight": noise(splits[4], (N_SECTION, D, PROJ), D ** -0.5, 0.21875, ((0, 2), (1, 4))),
        "dt_weight": noise(splits[5], (N_SECTION, D, HEADS), D ** -0.5, 0.21875, ((0, 2), (1, 4))),
        "conv_weight": noise(splits[6], (N_SECTION, CONV, XBC), CONV ** -0.5, 3.0, ((0, 2), (2, 4))),
        "conv_bias": noise(splits[7], (N_SECTION, XBC), 0.5, 3.0, ((0, 2), (1, 4))),
        "dt_bias": jnp.clip(-4.0 + 3.0 * jax.random.uniform(splits[8], (N_SECTION, HEADS), jnp.float32) ** block_scale(splits[8], (N_SECTION, HEADS), ((0, 2), (1, 4)), -0.2, 0.2), -4.0, -1.0).astype(jnp.bfloat16),
        "a_log": jnp.clip(-3.0 + 4.0 * jax.random.uniform(splits[9], (N_SECTION, HEADS), jnp.float32) ** block_scale(splits[9], (N_SECTION, HEADS), ((0, 2), (1, 4)), -0.2, 0.2), -3.0, 1.0).astype(jnp.bfloat16),
        "skip": jnp.clip(0.5 + 1.0 * jax.random.uniform(splits[10], (N_SECTION, HEADS), jnp.float32) ** block_scale(splits[10], (N_SECTION, HEADS), ((0, 2), (1, 4)), -0.2, 0.2), 0.5, 1.5).astype(jnp.bfloat16),
        "gated_gain": jnp.clip(1.0 + 0.18 * jax.random.normal(splits[11], (N_SECTION, INNER), jnp.float32), 0.099609375, 1.8984375).astype(jnp.bfloat16),
        "out_weight": noise(splits[12], (N_SECTION, INNER, D), INNER ** -0.5, 0.15625, ((0, 2), (1, 4))),
    }


@jax.custom_vjp
def low(v):
    return lax.optimization_barrier(v.astype(jnp.bfloat16)).astype(jnp.float32)

@jax.custom_vjp
def low_back(v):
    return v

def low_keep(v):
    return (low(v), None)

def low_pass(kept, grad):
    return (grad,)

def back_keep(v):
    return (v, None)

def back_low(kept, grad):
    return (low(grad),)
low.defvjp(low_keep, low_pass)
low_back.defvjp(back_keep, back_low)
EPS = 1e-05
HIGH = lax.Precision.HIGHEST

def mat_dot(left, right):
    return jnp.dot(left, right, precision=HIGH)

def state_scan(xs, bmat, cmat, rate, dt):
    length = xs.shape[0]
    block_len = min(SPAN, length)
    blocks = length // block_len
    xq = xs.reshape(blocks, block_len, HEADS, HEAD_DIM)
    bq = bmat.reshape(blocks, block_len, STATE)
    cq = cmat.reshape(blocks, block_len, STATE)
    rq = rate.reshape(blocks, block_len, HEADS)
    dq = dt.reshape(blocks, block_len, HEADS)
    lower = (jnp.arange(block_len)[:, None] >= jnp.arange(block_len)[None, :])[None, :, :]

    def block_step(state, inputs):
        xb, bb, cb, rb, db = inputs
        cum = jnp.cumsum(rb, axis=0)
        cum_t = cum.T
        diff = cum_t[:, :, None] - cum_t[:, None, :]
        decay = jnp.where(lower, jnp.exp(jnp.where(lower, diff, 0.0)), 0.0)
        inner = mat_dot(cb, bb.T)
        scores = low(inner[None, :, :] * decay * db.T[:, None, :])
        y_diag = jnp.einsum('hij,jhp->ihp', scores, xb, precision=HIGH)
        tail = jnp.exp(cum[-1][None, :] - cum) * db
        contrib = jnp.einsum('jh,jhp,jn->hpn', tail, xb, bb, precision=HIGH)
        y_off = jnp.einsum('in,hpn->ihp', cb, state, precision=HIGH) * jnp.exp(cum)[:, :, None]
        new_state = state * jnp.exp(cum[-1])[:, None, None] + contrib
        return (new_state, y_diag + y_off)
    start = jnp.zeros((HEADS, HEAD_DIM, STATE), jnp.float32)
    _, ys = lax.scan(jax.checkpoint(block_step), start, (xq, bq, cq, rq, dq))
    return ys.reshape(length, INNER)

def mixer_layer(x, weights, mask):
    g_in, w_in, w_dt, conv_w, conv_b, dt_b, a_log, skip_c, g_out, w_out = weights
    length = x.shape[0]
    h = low(x * lax.rsqrt(lax.optimization_barrier(jnp.mean(x * x, axis=-1, keepdims=True)) + EPS) * g_in)
    zx = low_back(mat_dot(h, w_in))
    raw = low_back(mat_dot(h, w_dt))
    gate = zx[:, :INNER]
    xbc = zx[:, INNER:]
    padded = jnp.concatenate([jnp.zeros((CONV - 1, XBC), jnp.float32), xbc], axis=0)
    conv = conv_b[None, :] + padded[0:length] * conv_w[0][None, :]
    for tap in range(1, CONV):
        conv = conv + padded[tap:tap + length] * conv_w[tap][None, :]
    act = jax.nn.silu(conv)
    xs = low(act[:, :INNER])
    bmat = low(act[:, INNER:INNER + STATE])
    cmat = low(act[:, INNER + STATE:])
    dt = jax.nn.softplus(raw + dt_b[None, :])
    rate = dt * (-jnp.exp(a_log))[None, :]
    y = state_scan(xs, bmat, cmat, rate, dt)
    y = y + xs * jnp.repeat(skip_c, HEAD_DIM)[None, :]
    gated = y * jax.nn.silu(gate)
    u = low(gated * lax.rsqrt(lax.optimization_barrier(jnp.mean(gated * gated, axis=-1, keepdims=True)) + EPS) * g_out)
    out = low_back(mat_dot(u, w_out))
    return (x + out) * mask[:, None]

def reference(tokens, cotangent, lengths, norm_gain, in_weight, dt_weight, conv_weight, conv_bias, dt_bias, a_log, skip, gated_gain, out_weight):
    weights = tuple((w.astype(jnp.float32) for w in (norm_gain, in_weight, dt_weight, conv_weight, conv_bias, dt_bias, a_log, skip, gated_gain, out_weight)))
    width = tokens.shape[2]
    count = tokens.shape[0] * (tokens.shape[1] // SEQ)
    seq_tokens = tokens.reshape(count, SEQ, width)
    seq_cot = cotangent.reshape(count, SEQ, width)
    seq_len = lengths.reshape(count).astype(jnp.int32)
    positions = jnp.arange(SEQ, dtype=jnp.int32)

    def one_sequence(carry, item):
        x_seq, cot_seq, seq_length = item
        mask = (positions < seq_length).astype(jnp.float32)

        def both_layers(x_in, probe, *w):
            first = tuple((a[0] for a in w))
            second = tuple((a[1] for a in w))
            y_first = mixer_layer(x_in, first, mask)
            v_in = low_back(low(y_first)) + probe
            y_second = mixer_layer(v_in, second, mask)
            return (y_second, y_first)
        zeros_in = jnp.zeros((SEQ, width), jnp.float32)
        (y_second, y_first), pull = jax.vjp(both_layers, x_seq.astype(jnp.float32), zeros_in, *weights)
        grads = pull((cot_seq.astype(jnp.float32), zeros_in))
        new_carry = tuple((c + g for c, g in zip(carry, grads[2:])))
        return (new_carry, (y_first.astype(jnp.bfloat16), y_second.astype(jnp.bfloat16), grads[0], grads[1]))
    start = tuple((jnp.zeros(w.shape, jnp.float32) for w in weights))
    totals, (firsts, seconds, dxs, dvs) = lax.scan(one_sequence, start, (seq_tokens, seq_cot, seq_len))
    shape_out = (2,) + tokens.shape
    section_outputs = jnp.stack([firsts, seconds]).reshape(shape_out)
    section_input_grads = jnp.stack([dxs, dvs]).reshape(shape_out)
    return (section_outputs, section_input_grads, totals[0], totals[1], totals[2], totals[3], totals[4], totals[5], totals[6], totals[7], totals[8], totals[9])
```

```python
import functools

import jax
import jax.numpy as jnp
from jax import lax
from jax.experimental import pallas as pl
from jax.experimental.pallas import tpu as pltpu
from jax.sharding import PartitionSpec as P

INNER = 1536
HEADS = 24
STATE = 128
HEAD_DIM = 64
CONV = 4
XBC = 1792
LANES = 128
TILE = 256
PAD = 8

EPS = 1e-05
F32 = jnp.float32
BF16 = jnp.bfloat16
ANY = pl.BlockSpec(memory_space=pl.ANY)
VMEM_LIMIT = 44 * 1024 * 1024


def mm(a, b, contract=(1, 0), precision=None):
    dims = (((contract[0],), (contract[1],)), ((), ()))
    return lax.dot_general(a, b, dims, precision=precision, preferred_element_type=F32)


def sigmoid(v):
    return 1.0 / (1.0 + jnp.exp(-v))


def split_two(v):
    high = v.astype(BF16)
    return high, (v - high.astype(F32)).astype(BF16)


class Copies:
    def __init__(self, sems):
        self.sems = sems
        self.used = 0

    def make(self, source, target):
        copy = pltpu.make_async_copy(source, target, self.sems.at[self.used])
        self.used += 1
        return copy

    def start(self, source, target):
        copy = self.make(source, target)
        copy.start()
        return copy


def on_section(where, section, body):
    if where == "all":
        body()
    elif where is not None:
        pl.when(section == (0 if where == "s0" else 1))(body)


def layer_kernel(cfg, *refs):
    names = cfg["names"]
    r = dict(zip(names, refs))
    n = cfg["pieces"]
    seq, width = cfg["seq"], cfg["width"]
    rows_in, rows_out = width // n, INNER // n
    meta = r["meta"]
    section, block, length = meta[0], meta[1], meta[2]
    order = [meta[3 + k] for k in range(n)]
    f_on, load_on, b_on, work_on = cfg["f_on"], cfg["load_on"], cfg["b_on"], cfg["work_on"]
    win, wout, wdt, pv = r["win_v"], r["wout_v"], r["wdt"], r["pv"]
    gate, xbc, y_s, raw_s, xs_s = r["gate_v"], r["xbc_v"], r["y_v"], r["raw_v"], r["xs_v"]
    inner_tiles = INNER // TILE
    conv_tiles = XBC // TILE
    pairs = INNER // LANES
    copies = Copies(r["sems"])

    def cols(k, size=TILE):
        return slice(k * size, (k + 1) * size)

    def body():
        if f_on is not None and cfg["has_arr"]:
            copy_x = copies.make(r["tok"].at[block], r["x_v"])
            other_x = pltpu.make_async_copy(r["arr"], r["x_v"], copies.sems.at[copies.used - 1])
            pl.when(section == 0)(copy_x.start)
            pl.when(section != 0)(other_x.start)
        else:
            copy_x = copies.start(r["tok"].at[block], r["x_v"])
        wait_in, wait_out = [], []
        for k in range(n):
            row = pl.multiple_of(order[k] * rows_in, 16)
            wait_in.append(copies.start(r[f"win{k}"], win.at[pl.ds(row, rows_in), :]))
        for k in range(n):
            row = pl.multiple_of(order[k] * rows_out, 16)
            wait_out.append(copies.start(r[f"wout{k}"], wout.at[pl.ds(row, rows_out), :]))
        copy_g = None
        if b_on is not None:
            copy_g = copies.make(r["cot"].at[block], r["g_v"])
            if cfg["has_arrg"]:
                other_g = pltpu.make_async_copy(r["arrg"], r["g_v"], copies.sems.at[copies.used - 1])
                pl.when(section == 1)(copy_g.start)
                pl.when(section != 1)(other_g.start)
            else:
                copy_g.start()
        loads = []
        if load_on is not None:
            loads = [
                copies.make(r["gate_i"], gate),
                copies.make(r["xbc_i"], xbc.at[PAD : PAD + seq, :]),
                copies.make(r["y_i"], y_s),
                copies.make(r["raw_i"], raw_s),
                copies.make(r["xs_i"], xs_s),
            ]

            def start_loads():
                for copy in loads:
                    copy.start()

            on_section(load_on, section, start_loads)

        below = lax.broadcasted_iota(jnp.int32, (seq, seq), 0) >= lax.broadcasted_iota(
            jnp.int32, (seq, seq), 1
        )
        row_id = lax.broadcasted_iota(jnp.int32, (seq, 1), 0)
        mask = jnp.where(row_id < length, 1.0, 0.0)
        lane = lax.broadcasted_iota(jnp.int32, (seq, LANES), 1)
        first_head = lane < HEAD_DIM
        xbc[0:PAD, :] = jnp.zeros((PAD, XBC), F32)
        copy_x.wait()
        x = r["x_v"][...].astype(F32)
        scale = lax.rsqrt(jnp.mean(x * x, axis=-1, keepdims=True) + EPS)
        gain = pv[6:7, 0:width]
        outs = []

        def save(name, source):
            if name in r:
                outs.append(copies.start(source, r[name]))

        def finish_outs():
            for copy in outs:
                copy.wait()
            outs.clear()

        def conv_tile(k):
            t = cols(k)
            conv = pv[4:5, t]
            for tap in range(CONV):
                start = PAD - (CONV - 1) + tap
                conv = conv + xbc[start : start + seq, t] * pv[tap : tap + 1, t]
            return conv

        def steps(value):
            v = value + pv[7:8, 0:LANES]
            small = jnp.exp(-jnp.abs(v))
            dt = jnp.maximum(v, 0.0) + jnp.log1p(small)
            minus_a = -jnp.exp(pv[7:8, LANES : 2 * LANES])
            rate = dt * minus_a
            ones = jnp.where(below, 1.0, 0.0)
            cum = mm(ones, rate, precision=lax.Precision.HIGHEST)
            return v, dt, minus_a, rate, cum

        def forward():
            h = (x * scale * gain).astype(BF16)
            for copy in wait_in:
                copy.wait()
            for k in range(inner_tiles):
                gate[:, cols(k)] = mm(h, win[:, cols(k)])
            for k in range(conv_tiles):
                t = slice(INNER + k * TILE, INNER + (k + 1) * TILE)
                xbc[PAD : PAD + seq, cols(k)] = mm(h, win[:, t])
            raw = mm(h, wdt[...])
            raw_s[...] = raw
            save("gate_o", gate)
            save("xbc_o", xbc.at[PAD : PAD + seq, :])
            save("raw_o", raw_s)
            h_t = h.T
            r["ht_v"][...] = h_t
            for k in range(conv_tiles):
                conv = conv_tile(k)
                xs_s[:, cols(k)] = (conv * sigmoid(conv)).astype(BF16)
            save("xs_o", xs_s)
            _, dt, _, _, cum = steps(raw)
            cum_t, dt_t = cum.T, dt.T
            bmat = xs_s[:, INNER : INNER + STATE]
            cmat = xs_s[:, INNER + STATE : XBC]
            inner = mm(cmat, bmat, (1, 1))
            total = jnp.zeros((seq, LANES), F32)
            gated_v = r["a_v"]
            for p in range(pairs):
                t = cols(p, LANES)
                both = []
                for head in (2 * p, 2 * p + 1):
                    diff = cum[:, head : head + 1] - cum_t[head : head + 1, :]
                    decay = jnp.exp(jnp.where(below, diff, -1e30))
                    both.append((inner * decay * dt_t[head : head + 1, :]).astype(BF16))
                xp = xs_s[:, t]
                none = jnp.zeros_like(xp)
                wide = jnp.concatenate(
                    [jnp.where(first_head, xp, none), jnp.where(first_head, none, xp)], axis=0
                )
                y = mm(jnp.concatenate(both, axis=1), wide) + xp.astype(F32) * pv[8:9, t]
                y_s[:, t] = y
                z = gate[:, t]
                gated = y * (z * sigmoid(z))
                gated_v[:, t] = gated
                total = total + gated * gated
            save("y_o", y_s)
            back = lax.rsqrt(jnp.sum(total, axis=-1, keepdims=True) / INNER + EPS)
            for p in range(inner_tiles):
                t = cols(p)
                u = (gated_v[:, t] * back * pv[5:6, t]).astype(BF16)
                r["u_v"][:, t] = u
                r["ut_v"][t, :] = u.T
            for copy in wait_out:
                copy.wait()
            for k in range(width // TILE):
                t = cols(k)
                value = x[:, t] + mm(r["u_v"][...], wout[:, t])
                r["out_v"][:, t] = (value * mask).astype(BF16)
            save("out_o", r["out_v"])
            for k in range(n):
                a = pl.multiple_of(order[k] * rows_in, 16)
                b = pl.multiple_of(order[k] * rows_out, 16)
                target = r[f"hu{k}_o"]
                outs.append(copies.start(r["ht_v"].at[pl.ds(a, rows_in), :], target.at[0:rows_in, :]))
                outs.append(
                    copies.start(
                        r["ut_v"].at[pl.ds(b, rows_out), :],
                        target.at[rows_in : rows_in + rows_out, :],
                    )
                )
            finish_outs()

        def ready():
            for copy in loads:
                copy.wait()
            for copy in wait_in + wait_out:
                copy.wait()

        def backward():
            copy_g.wait()
            g = r["g_v"][...].astype(F32) * mask
            r["dout_v"][...] = g.astype(BF16)
            save("dout_o", r["dout_v"])
            a_s, dact, dconv, dzx = r["a_v"], r["dact_v"], r["dconv_v"], r["dzx_v"]
            small = r["small_v"]
            small[...] = jnp.zeros(small.shape, F32)
            dconv[seq : seq + PAD, :] = jnp.zeros((PAD, XBC), F32)
            total = jnp.zeros((seq, TILE), F32)
            mixed = jnp.zeros((seq, TILE), F32)
            for k in range(inner_tiles):
                t = cols(k)
                du = mm(r["dout_v"][...], wout[t, :], (1, 1))
                a_s[:, t] = du
                z = gate[:, t]
                gated = y_s[:, t] * (z * sigmoid(z))
                total = total + gated * gated
                mixed = mixed + du * pv[5:6, t] * gated
            back = lax.rsqrt(jnp.sum(total, axis=-1, keepdims=True) / INNER + EPS)
            pull = jnp.sum(mixed, axis=-1, keepdims=True) / INNER * back * back
            for k in range(inner_tiles):
                t = cols(k)
                z, y, du = gate[:, t], y_s[:, t], a_s[:, t]
                sig = sigmoid(z)
                act = z * sig
                gated = y * act
                small[5:6, t] = jnp.sum(du * gated * back, axis=0, keepdims=True)
                dgated = back * (du * pv[5:6, t] - gated * pull)
                a_s[:, t] = dgated * act
                dzx[:, t] = (dgated * y * (sig * (1.0 + z * (1.0 - sig)))).astype(BF16)
            v, dt, minus_a, rate, cum = steps(raw_s[...])
            cum_t, dt_t = cum.T, dt.T
            bmat = xs_s[:, INNER : INNER + STATE]
            cmat = xs_s[:, INNER + STATE : XBC]
            inner = mm(cmat, bmat, (1, 1))
            dinner = jnp.zeros((seq, seq), F32)
            dcum = jnp.zeros((seq, LANES), F32)
            dlast = jnp.zeros((seq, LANES), F32)
            dskip = jnp.zeros((PAD, LANES), F32)
            head_row = lax.broadcasted_iota(jnp.int32, (2 * LANES, LANES), 0)
            head_col = lax.broadcasted_iota(jnp.int32, (2 * LANES, LANES), 1)
            for p in range(pairs):
                t = cols(p, LANES)
                both, decays = [], []
                for head in (2 * p, 2 * p + 1):
                    diff = cum[:, head : head + 1] - cum_t[head : head + 1, :]
                    decay = jnp.exp(jnp.where(below, diff, -1e30))
                    both.append((inner * decay * dt_t[head : head + 1, :]).astype(BF16))
                    decays.append(decay * dt_t[head : head + 1, :])
                scores = jnp.concatenate(both, axis=1)
                xp = xs_s[:, t]
                none = jnp.zeros_like(xp)
                wide = jnp.concatenate(
                    [jnp.where(first_head, xp, none), jnp.where(first_head, none, xp)], axis=0
                )
                dy = a_s[:, t]
                dy_low = dy.astype(BF16)
                dscores = mm(dy_low, wide, (1, 1))
                dinner = dinner + dscores[:, 0:seq] * decays[0] + dscores[:, seq:] * decays[1]
                spread = mm(scores, dy_low, (0, 0))
                dxs = jnp.where(first_head, spread[0:seq], spread[seq:])
                xf = xp.astype(F32)
                skip = pv[8:9, t]
                dact[:, t] = dy * skip + dxs
                own = jnp.where(head_col == 2 * p + (head_row % LANES) // HEAD_DIM, 1.0, 0.0).astype(BF16)
                left = xf * dxs
                dlast = dlast + mm(jnp.concatenate(split_two(left), axis=1), own)
                gap = dy_low.astype(F32) * (y_s[:, t] - skip * xf) - left
                dcum = dcum + mm(jnp.concatenate(split_two(gap), axis=1), own)
                by_lane = jnp.sum(dy * xf, axis=0, keepdims=True)
                by_lane = jnp.broadcast_to(by_lane, (PAD, LANES))
                dskip = dskip + mm(jnp.concatenate(split_two(by_lane), axis=1), own)
            above = jnp.where(
                lax.broadcasted_iota(jnp.int32, (seq, seq), 0)
                <= lax.broadcasted_iota(jnp.int32, (seq, seq), 1),
                1.0,
                0.0,
            )
            drate = mm(above, dcum, precision=lax.Precision.HIGHEST)
            sig = sigmoid(v)
            ratio = jnp.where(v < -15.0, 1.0, sig / jnp.maximum(dt, 1e-30))
            draw = drate * minus_a * sig + dlast * ratio
            draw_low = draw.astype(BF16)
            dzx[:, INNER + XBC : INNER + XBC + LANES] = draw_low
            small[7:8, 0:LANES] = jnp.sum(draw, axis=0, keepdims=True)
            small[7:8, LANES : 2 * LANES] = jnp.sum(drate * rate, axis=0, keepdims=True)
            small[7:8, 2 * LANES : 3 * LANES] = dskip[0:1, :]
            dinner_low = dinner.astype(BF16)
            dact[:, INNER : INNER + STATE] = mm(dinner_low, cmat, (0, 0))
            dact[:, INNER + STATE : XBC] = mm(dinner_low, bmat)
            for k in range(conv_tiles):
                t = cols(k)
                conv = conv_tile(k)
                sig = sigmoid(conv)
                grad = dact[:, t] * (sig * (1.0 + conv * (1.0 - sig)))
                dconv[0:seq, t] = grad
                small[4:5, t] = jnp.sum(grad, axis=0, keepdims=True)
                dxbc = jnp.zeros((seq, TILE), F32)
                for tap in range(CONV):
                    start = PAD - (CONV - 1) + tap
                    small[tap : tap + 1, t] = jnp.sum(
                        grad * xbc[start : start + seq, t], axis=0, keepdims=True
                    )
                    ahead = CONV - 1 - tap
                    dxbc = dxbc + dconv[ahead : ahead + seq, t] * pv[tap : tap + 1, t]
                dzx[:, INNER + k * TILE : INNER + (k + 1) * TILE] = dxbc.astype(BF16)
            save("dzx_o", dzx)
            dh = r["dh_v"]
            for k in range(width // TILE):
                t = cols(k)
                dh[:, t] = mm(dzx[:, 0 : INNER + XBC], win[t, :], (1, 1)) + mm(draw_low, wdt[t, :], (1, 1))
            product = dh[...] * gain
            pulled = jnp.mean(product * x, axis=-1, keepdims=True) * scale * scale
            dx = g + scale * (product - x * pulled)
            small[6:7, 0:width] = jnp.sum(dh[...] * x * scale, axis=0, keepdims=True)
            dh[...] = dx
            r["dxb_v"][...] = dx.astype(BF16)
            save("dxb_o", r["dxb_v"])
            save("dx_o", dh)
            save("small_o", small)
            finish_outs()

        if f_on is not None:
            on_section(f_on, section, forward)
        if load_on is not None:
            on_section(load_on, section, ready)
        if b_on is not None:
            if f_on == "all" and b_on != "all":

                def drain():
                    copy_g.wait()

                on_section("s0" if b_on == "s1" else "s1", section, drain)
            on_section(b_on, section, backward)

    on_section(work_on, section, body)


RESIDUALS = ("gate", "xbc", "y", "raw", "xs")


def layer_call(
    name, f_on, load_on, b_on, work_on, meta, tok, cot, arr, arrg, weights, residual, kept, save_residual
):
    win, wout, wdt, pv = weights
    n = len(win)
    seq, width = tok.shape[1], tok.shape[2]
    rows = width // n + INNER // n
    proj = INNER + XBC
    shapes = dict(
        gate=((seq, INNER), F32),
        xbc=((seq, XBC), F32),
        y=((seq, INNER), F32),
        raw=((seq, LANES), F32),
        xs=((seq, XBC), BF16),
        out=((seq, width), BF16),
        dout=((seq, width), BF16),
        dzx=((seq, proj + LANES), BF16),
        dx=((seq, width), F32),
        dxb=((seq, width), BF16),
        small=((8, XBC), F32),
    )
    for k in range(n):
        shapes[f"hu{k}"] = ((rows, seq), BF16)
    whole = pl.BlockSpec(memory_space=pltpu.VMEM)
    inputs = [("meta", meta, pl.BlockSpec(memory_space=pltpu.SMEM)), ("tok", tok, ANY)]
    if b_on is not None:
        inputs.append(("cot", cot, ANY))
    if arr is not None:
        inputs.append(("arr", arr, ANY))
    if arrg is not None:
        inputs.append(("arrg", arrg, ANY))
    inputs += [(f"win{k}", w, ANY) for k, w in enumerate(win)]
    inputs += [(f"wout{k}", w, ANY) for k, w in enumerate(wout)]
    inputs += [("wdt", wdt, whole), ("pv", pv, whole)]
    if load_on is not None:
        inputs += [(f"{k}_i", residual[k], ANY) for k in RESIDUALS]
    outputs = []
    if f_on is not None:
        outputs += ["out"] + [f"hu{k}" for k in range(n)]
        if save_residual:
            outputs += list(RESIDUALS)
    if b_on is not None:
        outputs += ["dout", "dzx", "dx", "dxb", "small"]
    aliases = {}
    for place, key in enumerate(outputs):
        if key in kept:
            aliases[len(inputs)] = place
            inputs.append((f"{key}_k", kept[key], ANY))
    scratch = dict(
        x_v=((seq, width), BF16),
        g_v=((seq, width), BF16),
        dout_v=((seq, width), BF16),
        out_v=((seq, width), BF16),
        dxb_v=((seq, width), BF16),
        win_v=((width, proj), BF16),
        wout_v=((INNER, width), BF16),
        gate_v=((seq, INNER), F32),
        xbc_v=((seq + PAD, XBC), F32),
        y_v=((seq, INNER), F32),
        raw_v=((seq, LANES), F32),
        xs_v=((seq, XBC), BF16),
        ht_v=((width, seq), BF16),
        u_v=((seq, INNER), BF16),
        ut_v=((INNER, seq), BF16),
        a_v=((seq, INNER), F32),
        dact_v=((seq, XBC), F32),
        dconv_v=((seq + PAD, XBC), F32),
        dzx_v=((seq, proj + LANES), BF16),
        dh_v=((seq, width), F32),
        small_v=((8, XBC), F32),
    )
    names = [k for k, _, _ in inputs] + [f"{k}_o" for k in outputs] + list(scratch) + ["sems"]
    cfg = dict(
        names=names,
        pieces=n,
        seq=seq,
        width=width,
        f_on=f_on,
        load_on=load_on,
        b_on=b_on,
        work_on=work_on,
        has_arr=arr is not None,
        has_arrg=arrg is not None,
    )
    results = pl.pallas_call(
        functools.partial(layer_kernel, cfg),
        out_shape=[jax.ShapeDtypeStruct(*shapes[k]) for k in outputs],
        in_specs=[spec for _, _, spec in inputs],
        out_specs=[ANY for _ in outputs],
        scratch_shapes=[pltpu.VMEM(*v) for v in scratch.values()]
        + [pltpu.SemaphoreType.DMA((4 * n + 32,))],
        input_output_aliases=aliases,
        compiler_params=pltpu.CompilerParams(vmem_limit_bytes=VMEM_LIMIT),
        name=name,
    )(*[value for _, value, _ in inputs])
    return dict(zip(outputs, results))


def across(block, axis, way):
    size = lax.axis_size(axis)
    route = [(i, i + way) for i in range(size) if 0 <= i + way < size]
    return lax.ppermute(block, axis, route)


def on_device(
    tokens,
    cotangent,
    lengths,
    norm_gain,
    in_weight,
    dt_weight,
    conv_weight,
    conv_bias,
    dt_bias,
    a_log,
    skip,
    gated_gain,
    out_weight,
):
    n = lax.axis_size("fsdp")
    section = lax.axis_index("section")
    seq, width = tokens.shape[1], tokens.shape[2]
    proj = INNER + XBC
    smalls = (norm_gain, conv_weight, conv_bias, dt_bias, a_log, skip, gated_gain, dt_weight)
    packed = jnp.concatenate([s[0].reshape(-1) for s in smalls])
    packed = lax.all_gather(packed, "fsdp", axis=0)
    parts, place = [], 0
    for s in smalls:
        size = s.size
        parts.append(packed[:, place : place + size].reshape((n,) + s.shape[1:]))
        place += size

    def row(v, size=XBC):
        v = v.reshape(1, -1).astype(F32)
        return jnp.pad(v, ((0, 0), (0, size - v.shape[1])))

    conv_w = parts[1].transpose(1, 0, 2).reshape(CONV, XBC).astype(F32)
    sevens = jnp.concatenate([row(parts[3], LANES), row(parts[4], LANES), row(parts[5], LANES)], axis=1)
    pv = jnp.concatenate(
        [
            conv_w,
            row(parts[2]),
            row(parts[6]),
            row(parts[0]),
            row(sevens),
            row(jnp.repeat(parts[5].reshape(-1), HEAD_DIM)),
            jnp.zeros((7, XBC), F32),
        ]
    )
    wdt = jnp.pad(parts[7].reshape(width, HEADS), ((0, 0), (0, LANES - HEADS)))
    full_in = lax.all_gather(in_weight[0], "fsdp", axis=0, tiled=True)
    full_out = lax.all_gather(out_weight[0], "fsdp", axis=0, tiled=True)
    weights = ([full_in], [full_out], wdt, pv)
    pieces = 1
    order = jnp.zeros((pieces,), jnp.int32)

    def meta_of(block):
        return jnp.concatenate(
            [
                jnp.stack([section.astype(jnp.int32), block.astype(jnp.int32), lengths[block, 0]]),
                order,
            ]
        )

    meta_p, meta_q = meta_of(section), meta_of(1 - section)
    first = layer_call(
        "first", "s0", None, None, "s0", meta_p, tokens, None, None, None, weights, None, {}, True
    )
    arr_q = across(first["out"], "section", 1)
    second = layer_call(
        "second", "all", None, "s1", "all", meta_q, tokens, cotangent, arr_q, None, weights, None, {}, True
    )
    arr_p = across(second["out"], "section", 1)
    arrg_p = across(second["dxb"], "section", -1)
    third = layer_call(
        "third", "s1", "s0", "all", "all", meta_p, tokens, cotangent, arr_p, arrg_p, weights, first,
        {k: first[k] for k in first if k not in RESIDUALS}, False,
    )
    arrg_q = across(third["dxb"], "section", -1)
    fourth = layer_call(
        "fourth", None, "s0", "s0", "s0", meta_q, tokens, cotangent, None, arrg_q, weights, second,
        {k: second[k] for k in ("dout", "dzx", "dx", "dxb", "small")}, False,
    )
    at_zero = section == 0

    def by_block(p, q):
        return jnp.stack([jnp.where(at_zero, p, q), jnp.where(at_zero, q, p)])

    outputs = by_block(third["out"], second["out"])
    input_grads = by_block(third["dx"], fourth["dx"])
    small = third["small"] + fourth["small"]
    rows_in, rows_out = width // pieces, INNER // pieces
    left = jnp.concatenate([third["hu0"], second["hu0"]], axis=1)
    right = jnp.concatenate([third["dzx"], fourth["dzx"]], axis=0)
    dout = jnp.concatenate([third["dout"], fourth["dout"]], axis=0)
    grad_in = jnp.dot(left[:rows_in], right, preferred_element_type=F32).astype(BF16)
    grad_out = jnp.dot(left[rows_in:], dout, preferred_element_type=F32).astype(BF16)
    grad_in = lax.psum_scatter(grad_in, "fsdp", scatter_dimension=0, tiled=True)
    grad_out = lax.psum_scatter(grad_out, "fsdp", scatter_dimension=0, tiled=True)
    grad_in, grad_out = lax.psum((grad_in, grad_out), "dp")
    small = lax.psum(small, ("dp", "fsdp"))
    me = lax.axis_index("fsdp")

    def own(v):
        size = v.shape[-1] // n
        return lax.dynamic_slice_in_dim(v, me * size, size, axis=v.ndim - 1)

    return (
        outputs[None],
        input_grads[None],
        own(small[6:7, :width]),
        grad_in[None, :, :proj].astype(F32),
        grad_in[None, :, proj : proj + HEADS].astype(F32),
        own(small[None, 0:CONV]),
        own(small[4:5]),
        own(small[7:8, 0:HEADS]),
        own(small[7:8, LANES : LANES + HEADS]),
        own(small[7:8, 2 * LANES : 2 * LANES + HEADS]),
        own(small[5:6, :INNER]),
        grad_out[None].astype(F32),
    )


def solution(mesh):
    in_specs = (
        P(None, ("dp", "fsdp"), None),
        P(None, ("dp", "fsdp"), None),
        P(None, ("dp", "fsdp")),
        P("section", "fsdp"),
        P("section", "fsdp", None),
        P("section", "fsdp", None),
        P("section", None, "fsdp"),
        P("section", "fsdp"),
        P("section", "fsdp"),
        P("section", "fsdp"),
        P("section", "fsdp"),
        P("section", "fsdp"),
        P("section", "fsdp", None),
    )
    out_specs = (
        P("section", None, ("dp", "fsdp"), None),
        P("section", None, ("dp", "fsdp"), None),
        P("section", "fsdp"),
        P("section", "fsdp", None),
        P("section", "fsdp", None),
        P("section", None, "fsdp"),
        P("section", "fsdp"),
        P("section", "fsdp"),
        P("section", "fsdp"),
        P("section", "fsdp"),
        P("section", "fsdp"),
        P("section", "fsdp", None),
    )
    return jax.shard_map(
        on_device, mesh=mesh, in_specs=in_specs, out_specs=out_specs, check_vma=False
    )
```

```python
import functools

import jax
import jax.numpy as jnp
from jax import lax
from jax.experimental import pallas as pl
from jax.experimental.pallas import tpu as pltpu
from jax.sharding import PartitionSpec as P

INNER = 1536
HEADS = 24
STATE = 128
HEAD_DIM = 64
CONV = 4
XBC = 1792
LANES = 128
TILE = 256
PAD = 8

EPS = 1e-05
F32 = jnp.float32
BF16 = jnp.bfloat16
ANY = pl.BlockSpec(memory_space=pl.ANY)
VMEM_LIMIT = 44 * 1024 * 1024


def mm(a, b, contract=(1, 0), precision=None):
    dims = (((contract[0],), (contract[1],)), ((), ()))
    return lax.dot_general(a, b, dims, precision=precision, preferred_element_type=F32)


def sigmoid(v):
    return 1.0 / (1.0 + jnp.exp(-v))


def split_two(v):
    high = v.astype(BF16)
    return high, (v - high.astype(F32)).astype(BF16)


class Copies:
    def __init__(self, sems):
        self.sems = sems
        self.used = 0

    def make(self, source, target):
        copy = pltpu.make_async_copy(source, target, self.sems.at[self.used])
        self.used += 1
        return copy

    def start(self, source, target):
        copy = self.make(source, target)
        copy.start()
        return copy


def on_section(where, section, body):
    if where == "all":
        body()
    elif where is not None:
        pl.when(section == (0 if where == "s0" else 1))(body)


def layer_kernel(cfg, *refs):
    names = cfg["names"]
    r = dict(zip(names, refs))
    n = cfg["pieces"]
    seq, width = cfg["seq"], cfg["width"]
    rows_in, rows_out = width // n, INNER // n
    meta = r["meta"]
    section, block, length = meta[0], meta[1], meta[2]
    order = [meta[3 + k] for k in range(n)]
    f_on, load_on, b_on, work_on = cfg["f_on"], cfg["load_on"], cfg["b_on"], cfg["work_on"]
    win, wout, wdt, pv = r["win_v"], r["wout_v"], r["wdt"], r["pv"]
    gate, xbc, y_s, raw_s, xs_s = r["gate_v"], r["xbc_v"], r["y_v"], r["raw_v"], r["xs_v"]
    inner_tiles = INNER // TILE
    conv_tiles = XBC // TILE
    pairs = INNER // LANES
    copies = Copies(r["sems"])

    def cols(k, size=TILE):
        return slice(k * size, (k + 1) * size)

    def body():
        if f_on is not None and cfg["has_arr"]:
            copy_x = copies.make(r["tok"].at[block], r["x_v"])
            other_x = pltpu.make_async_copy(r["arr"], r["x_v"], copies.sems.at[copies.used - 1])
            pl.when(section == 0)(copy_x.start)
            pl.when(section != 0)(other_x.start)
        else:
            copy_x = copies.start(r["tok"].at[block], r["x_v"])
        wait_in, wait_out = [], []
        for k in range(n):
            row = pl.multiple_of(order[k] * rows_in, 16)
            wait_in.append(copies.start(r[f"win{k}"], win.at[pl.ds(row, rows_in), :]))
        for k in range(n):
            row = pl.multiple_of(order[k] * rows_out, 16)
            wait_out.append(copies.start(r[f"wout{k}"], wout.at[pl.ds(row, rows_out), :]))
        copy_g = None
        if b_on is not None:
            copy_g = copies.make(r["cot"].at[block], r["g_v"])
            if cfg["has_arrg"]:
                other_g = pltpu.make_async_copy(r["arrg"], r["g_v"], copies.sems.at[copies.used - 1])
                pl.when(section == 1)(copy_g.start)
                pl.when(section != 1)(other_g.start)
            else:
                copy_g.start()
        loads = []
        if load_on is not None:
            loads = [
                copies.make(r["gate_i"], gate),
                copies.make(r["xbc_i"], xbc.at[PAD : PAD + seq, :]),
                copies.make(r["y_i"], y_s),
                copies.make(r["raw_i"], raw_s),
                copies.make(r["xs_i"], xs_s),
            ]

            def start_loads():
                for copy in loads:
                    copy.start()

            on_section(load_on, section, start_loads)

        below = lax.broadcasted_iota(jnp.int32, (seq, seq), 0) >= lax.broadcasted_iota(
            jnp.int32, (seq, seq), 1
        )
        row_id = lax.broadcasted_iota(jnp.int32, (seq, 1), 0)
        mask = jnp.where(row_id < length, 1.0, 0.0)
        lane = lax.broadcasted_iota(jnp.int32, (seq, LANES), 1)
        first_head = lane < HEAD_DIM
        xbc[0:PAD, :] = jnp.zeros((PAD, XBC), F32)
        copy_x.wait()
        x = r["x_v"][...].astype(F32)
        scale = lax.rsqrt(jnp.mean(x * x, axis=-1, keepdims=True) + EPS)
        gain = pv[6:7, 0:width]
        outs = []

        def save(name, source):
            if name in r:
                outs.append(copies.start(source, r[name]))

        def finish_outs():
            for copy in outs:
                copy.wait()
            outs.clear()

        def conv_tile(k):
            t = cols(k)
            conv = pv[4:5, t]
            for tap in range(CONV):
                start = PAD - (CONV - 1) + tap
                conv = conv + xbc[start : start + seq, t] * pv[tap : tap + 1, t]
            return conv

        def steps(value):
            v = value + pv[7:8, 0:LANES]
            small = jnp.exp(-jnp.abs(v))
            dt = jnp.maximum(v, 0.0) + jnp.log1p(small)
            minus_a = -jnp.exp(pv[7:8, LANES : 2 * LANES])
            rate = dt * minus_a
            ones = jnp.where(below, 1.0, 0.0)
            cum = mm(ones, rate, precision=lax.Precision.HIGHEST)
            return v, dt, minus_a, rate, cum

        def forward():
            h = (x * scale * gain).astype(BF16)
            for copy in wait_in:
                copy.wait()
            for k in range(inner_tiles):
                gate[:, cols(k)] = mm(h, win[:, cols(k)])
            for k in range(conv_tiles):
                t = slice(INNER + k * TILE, INNER + (k + 1) * TILE)
                xbc[PAD : PAD + seq, cols(k)] = mm(h, win[:, t])
            raw = mm(h, wdt[...])
            raw_s[...] = raw
            save("gate_o", gate)
            save("xbc_o", xbc.at[PAD : PAD + seq, :])
            save("raw_o", raw_s)
            h_t = h.T
            r["ht_v"][...] = h_t
            for k in range(conv_tiles):
                conv = conv_tile(k)
                xs_s[:, cols(k)] = (conv * sigmoid(conv)).astype(BF16)
            save("xs_o", xs_s)
            _, dt, _, _, cum = steps(raw)
            cum_t, dt_t = cum.T, dt.T
            bmat = xs_s[:, INNER : INNER + STATE]
            cmat = xs_s[:, INNER + STATE : XBC]
            inner = mm(cmat, bmat, (1, 1))
            total = jnp.zeros((seq, LANES), F32)
            gated_v = r["a_v"]
            for p in range(pairs):
                t = cols(p, LANES)
                both = []
                for head in (2 * p, 2 * p + 1):
                    diff = cum[:, head : head + 1] - cum_t[head : head + 1, :]
                    decay = jnp.exp(jnp.where(below, diff, -1e30))
                    both.append((inner * decay * dt_t[head : head + 1, :]).astype(BF16))
                xp = xs_s[:, t]
                none = jnp.zeros_like(xp)
                wide = jnp.concatenate(
                    [jnp.where(first_head, xp, none), jnp.where(first_head, none, xp)], axis=0
                )
                y = mm(jnp.concatenate(both, axis=1), wide) + xp.astype(F32) * pv[8:9, t]
                y_s[:, t] = y
                z = gate[:, t]
                gated = y * (z * sigmoid(z))
                gated_v[:, t] = gated
                total = total + gated * gated
            save("y_o", y_s)
            back = lax.rsqrt(jnp.sum(total, axis=-1, keepdims=True) / INNER + EPS)
            for p in range(inner_tiles):
                t = cols(p)
                u = (gated_v[:, t] * back * pv[5:6, t]).astype(BF16)
                r["u_v"][:, t] = u
                r["ut_v"][t, :] = u.T
            for copy in wait_out:
                copy.wait()
            for k in range(width // TILE):
                t = cols(k)
                value = x[:, t] + mm(r["u_v"][...], wout[:, t])
                r["out_v"][:, t] = (value * mask).astype(BF16)
            save("out_o", r["out_v"])
            for k in range(n):
                a = pl.multiple_of(order[k] * rows_in, 16)
                b = pl.multiple_of(order[k] * rows_out, 16)
                target = r[f"hu{k}_o"]
                place = slice(cfg["slot"] * seq, (cfg["slot"] + 1) * seq)
                outs.append(
                    copies.start(r["ht_v"].at[pl.ds(a, rows_in), :], target.at[0:rows_in, place])
                )
                outs.append(
                    copies.start(
                        r["ut_v"].at[pl.ds(b, rows_out), :],
                        target.at[rows_in : rows_in + rows_out, place],
                    )
                )
            finish_outs()

        def ready():
            for copy in loads:
                copy.wait()
            for copy in wait_in + wait_out:
                copy.wait()

        def backward():
            copy_g.wait()
            g = r["g_v"][...].astype(F32) * mask
            r["dout_v"][...] = g.astype(BF16)
            if "all_o" in r:
                outs.append(copies.start(r["dout_v"], r["all_o"].at[:, 0:width]))
            a_s, dact, dconv, dzx = r["a_v"], r["dact_v"], r["dconv_v"], r["dzx_v"]
            small = r["small_v"]
            small[...] = jnp.zeros(small.shape, F32)
            dconv[seq : seq + PAD, :] = jnp.zeros((PAD, XBC), F32)
            total = jnp.zeros((seq, TILE), F32)
            mixed = jnp.zeros((seq, TILE), F32)
            for k in range(inner_tiles):
                t = cols(k)
                du = mm(r["dout_v"][...], wout[t, :], (1, 1))
                a_s[:, t] = du
                z = gate[:, t]
                gated = y_s[:, t] * (z * sigmoid(z))
                total = total + gated * gated
                mixed = mixed + du * pv[5:6, t] * gated
            back = lax.rsqrt(jnp.sum(total, axis=-1, keepdims=True) / INNER + EPS)
            pull = jnp.sum(mixed, axis=-1, keepdims=True) / INNER * back * back
            for k in range(inner_tiles):
                t = cols(k)
                z, y, du = gate[:, t], y_s[:, t], a_s[:, t]
                sig = sigmoid(z)
                act = z * sig
                gated = y * act
                small[5:6, t] = jnp.sum(du * gated * back, axis=0, keepdims=True)
                dgated = back * (du * pv[5:6, t] - gated * pull)
                a_s[:, t] = dgated * act
                dzx[:, t] = (dgated * y * (sig * (1.0 + z * (1.0 - sig)))).astype(BF16)
            if "all_o" in r:
                target = r["all_o"].at[:, width : width + INNER]
                outs.append(copies.start(dzx.at[:, 0:INNER], target))
            else:
                outs.append(copies.start(dzx.at[:, 0:INNER], r["dgate_o"]))
            v, dt, minus_a, rate, cum = steps(raw_s[...])
            cum_t, dt_t = cum.T, dt.T
            bmat = xs_s[:, INNER : INNER + STATE]
            cmat = xs_s[:, INNER + STATE : XBC]
            inner = mm(cmat, bmat, (1, 1))
            dinner = jnp.zeros((seq, seq), F32)
            dcum = jnp.zeros((seq, LANES), F32)
            dlast = jnp.zeros((seq, LANES), F32)
            dskip = jnp.zeros((PAD, LANES), F32)
            head_row = lax.broadcasted_iota(jnp.int32, (2 * LANES, LANES), 0)
            head_col = lax.broadcasted_iota(jnp.int32, (2 * LANES, LANES), 1)
            for p in range(pairs):
                t = cols(p, LANES)
                both, decays = [], []
                for head in (2 * p, 2 * p + 1):
                    diff = cum[:, head : head + 1] - cum_t[head : head + 1, :]
                    decay = jnp.exp(jnp.where(below, diff, -1e30))
                    both.append((inner * decay * dt_t[head : head + 1, :]).astype(BF16))
                    decays.append(decay * dt_t[head : head + 1, :])
                scores = jnp.concatenate(both, axis=1)
                xp = xs_s[:, t]
                none = jnp.zeros_like(xp)
                wide = jnp.concatenate(
                    [jnp.where(first_head, xp, none), jnp.where(first_head, none, xp)], axis=0
                )
                dy = a_s[:, t]
                dy_low = dy.astype(BF16)
                dscores = mm(dy_low, wide, (1, 1))
                dinner = dinner + dscores[:, 0:seq] * decays[0] + dscores[:, seq:] * decays[1]
                spread = mm(scores, dy_low, (0, 0))
                dxs = jnp.where(first_head, spread[0:seq], spread[seq:])
                xf = xp.astype(F32)
                skip = pv[8:9, t]
                dact[:, t] = dy * skip + dxs
                own = jnp.where(head_col == 2 * p + (head_row % LANES) // HEAD_DIM, 1.0, 0.0).astype(BF16)
                left = xf * dxs
                dlast = dlast + mm(jnp.concatenate(split_two(left), axis=1), own)
                gap = dy_low.astype(F32) * (y_s[:, t] - skip * xf) - left
                dcum = dcum + mm(jnp.concatenate(split_two(gap), axis=1), own)
                by_lane = jnp.sum(dy * xf, axis=0, keepdims=True)
                by_lane = jnp.broadcast_to(by_lane, (PAD, LANES))
                dskip = dskip + mm(jnp.concatenate(split_two(by_lane), axis=1), own)
            above = jnp.where(
                lax.broadcasted_iota(jnp.int32, (seq, seq), 0)
                <= lax.broadcasted_iota(jnp.int32, (seq, seq), 1),
                1.0,
                0.0,
            )
            drate = mm(above, dcum, precision=lax.Precision.HIGHEST)
            sig = sigmoid(v)
            ratio = jnp.where(v < -15.0, 1.0, sig / jnp.maximum(dt, 1e-30))
            draw = drate * minus_a * sig + dlast * ratio
            draw_low = draw.astype(BF16)
            dzx[:, INNER + XBC : INNER + XBC + LANES] = draw_low
            small[7:8, 0:LANES] = jnp.sum(draw, axis=0, keepdims=True)
            small[7:8, LANES : 2 * LANES] = jnp.sum(drate * rate, axis=0, keepdims=True)
            small[7:8, 2 * LANES : 3 * LANES] = dskip[0:1, :]
            dinner_low = dinner.astype(BF16)
            dact[:, INNER : INNER + STATE] = mm(dinner_low, cmat, (0, 0))
            dact[:, INNER + STATE : XBC] = mm(dinner_low, bmat)
            for k in range(conv_tiles):
                t = cols(k)
                conv = conv_tile(k)
                sig = sigmoid(conv)
                grad = dact[:, t] * (sig * (1.0 + conv * (1.0 - sig)))
                dconv[0:seq, t] = grad
                small[4:5, t] = jnp.sum(grad, axis=0, keepdims=True)
                dxbc = jnp.zeros((seq, TILE), F32)
                for tap in range(CONV):
                    start = PAD - (CONV - 1) + tap
                    small[tap : tap + 1, t] = jnp.sum(
                        grad * xbc[start : start + seq, t], axis=0, keepdims=True
                    )
                    ahead = CONV - 1 - tap
                    dxbc = dxbc + dconv[ahead : ahead + seq, t] * pv[tap : tap + 1, t]
                dzx[:, INNER + k * TILE : INNER + (k + 1) * TILE] = dxbc.astype(BF16)
            if "all_o" in r:
                target = r["all_o"].at[:, width + INNER : width + INNER + XBC + LANES]
                outs.append(copies.start(dzx.at[:, INNER : INNER + XBC + LANES], target))
            else:
                outs.append(copies.start(dzx.at[:, INNER : INNER + XBC + LANES], r["dside_o"]))
            dh = r["dh_v"]
            for k in range(width // TILE):
                t = cols(k)
                dh[:, t] = mm(dzx[:, 0 : INNER + XBC], win[t, :], (1, 1)) + mm(draw_low, wdt[t, :], (1, 1))
            product = dh[...] * gain
            pulled = jnp.mean(product * x, axis=-1, keepdims=True) * scale * scale
            dx = g + scale * (product - x * pulled)
            small[6:7, 0:width] = jnp.sum(dh[...] * x * scale, axis=0, keepdims=True)
            dh[...] = dx
            r["dxb_v"][...] = dx.astype(BF16)
            save("dxb_o", r["dxb_v"])
            save("dx_o", dh)
            save("small_o", small)
            finish_outs()

        if f_on is not None:
            on_section(f_on, section, forward)
        if load_on is not None:
            on_section(load_on, section, ready)
        if b_on is not None:
            if f_on == "all" and b_on != "all":

                def drain():
                    copy_g.wait()

                on_section("s0" if b_on == "s1" else "s1", section, drain)
            on_section(b_on, section, backward)

    on_section(work_on, section, body)


RESIDUALS = ("gate", "xbc", "y", "raw", "xs")


def layer_call(
    name,
    slot,
    f_on,
    load_on,
    b_on,
    work_on,
    meta,
    tok,
    cot,
    arr,
    arrg,
    weights,
    residual,
    kept,
    save_residual,
    one_array,
):
    win, wout, wdt, pv = weights
    n = len(win)
    seq, width = tok.shape[1], tok.shape[2]
    rows = width // n + INNER // n
    proj = INNER + XBC
    shapes = dict(
        gate=((seq, INNER), F32),
        xbc=((seq, XBC), F32),
        y=((seq, INNER), F32),
        raw=((seq, LANES), F32),
        xs=((seq, XBC), BF16),
        out=((seq, width), BF16),
        all=((seq, width + proj + LANES), BF16),
        dgate=((seq, INNER), BF16),
        dside=((seq, XBC + LANES), BF16),
        dx=((seq, width), F32),
        dxb=((seq, width), BF16),
        small=((8, XBC), F32),
    )
    for k in range(n):
        shapes[f"hu{k}"] = ((rows, 2 * seq), BF16)
    whole = pl.BlockSpec(memory_space=pltpu.VMEM)
    inputs = [("meta", meta, pl.BlockSpec(memory_space=pltpu.SMEM)), ("tok", tok, ANY)]
    if b_on is not None:
        inputs.append(("cot", cot, ANY))
    if arr is not None:
        inputs.append(("arr", arr, ANY))
    if arrg is not None:
        inputs.append(("arrg", arrg, ANY))
    inputs += [(f"win{k}", w, ANY) for k, w in enumerate(win)]
    inputs += [(f"wout{k}", w, ANY) for k, w in enumerate(wout)]
    inputs += [("wdt", wdt, whole), ("pv", pv, whole)]
    if load_on is not None:
        inputs += [(f"{k}_i", residual[k], ANY) for k in RESIDUALS]
    outputs = []
    if f_on is not None:
        outputs += ["out"] + [f"hu{k}" for k in range(n)]
        if save_residual:
            outputs += list(RESIDUALS)
    if b_on is not None:
        outputs += ["all"] if one_array else ["dgate", "dside"]
        outputs += ["dx", "dxb", "small"]
    aliases = {}
    for place, key in enumerate(outputs):
        if key in kept:
            aliases[len(inputs)] = place
            inputs.append((f"{key}_k", kept[key], ANY))
    scratch = dict(
        x_v=((seq, width), BF16),
        g_v=((seq, width), BF16),
        dout_v=((seq, width), BF16),
        out_v=((seq, width), BF16),
        dxb_v=((seq, width), BF16),
        win_v=((width, proj), BF16),
        wout_v=((INNER, width), BF16),
        gate_v=((seq, INNER), F32),
        xbc_v=((seq + PAD, XBC), F32),
        y_v=((seq, INNER), F32),
        raw_v=((seq, LANES), F32),
        xs_v=((seq, XBC), BF16),
        ht_v=((width, seq), BF16),
        u_v=((seq, INNER), BF16),
        ut_v=((INNER, seq), BF16),
        a_v=((seq, INNER), F32),
        dact_v=((seq, XBC), F32),
        dconv_v=((seq + PAD, XBC), F32),
        dzx_v=((seq, proj + LANES), BF16),
        dh_v=((seq, width), F32),
        small_v=((8, XBC), F32),
    )
    names = [k for k, _, _ in inputs] + [f"{k}_o" for k in outputs] + list(scratch) + ["sems"]
    cfg = dict(
        names=names,
        pieces=n,
        slot=slot,
        seq=seq,
        width=width,
        f_on=f_on,
        load_on=load_on,
        b_on=b_on,
        work_on=work_on,
        has_arr=arr is not None,
        has_arrg=arrg is not None,
    )
    results = pl.pallas_call(
        functools.partial(layer_kernel, cfg),
        out_shape=[jax.ShapeDtypeStruct(*shapes[k]) for k in outputs],
        in_specs=[spec for _, _, spec in inputs],
        out_specs=[ANY for _ in outputs],
        scratch_shapes=[pltpu.VMEM(*v) for v in scratch.values()]
        + [pltpu.SemaphoreType.DMA((4 * n + 32,))],
        input_output_aliases=aliases,
        compiler_params=pltpu.CompilerParams(vmem_limit_bytes=VMEM_LIMIT),
        name=name,
    )(*[value for _, value, _ in inputs])
    return dict(zip(outputs, results))


def product_kernel(rows, places, count, *refs):
    lefts, first, second = refs[:count], refs[count : 2 * count], refs[2 * count : 3 * count]
    out, left_v, right_v, sems = refs[3 * count :]
    seq = first[0].shape[0]
    copies = Copies(sems)
    waits = []
    for k in range(count):
        start = 2 * k * seq
        waits.append(copies.start(lefts[k].at[rows, :], left_v.at[:, start : start + 2 * seq]))
        waits.append(copies.start(first[k].at[:, places], right_v.at[start : start + seq, :]))
        waits.append(copies.start(second[k], right_v.at[start + seq : start + 2 * seq, :]))
    for copy in waits:
        copy.wait()
    size = out.shape[1]
    for k in range(0, size, TILE):
        t = slice(k, min(k + TILE, size))
        out[:, t] = mm(left_v[...], right_v[:, t]).astype(out.dtype)


def weight_product(name, lefts, rows, first, places, second):
    count = len(lefts)
    depth = 2 * count * first[0].shape[0]
    height, size = rows.stop - rows.start, places.stop - places.start
    return pl.pallas_call(
        functools.partial(product_kernel, rows, places, count),
        out_shape=jax.ShapeDtypeStruct((height, size), BF16),
        in_specs=[ANY] * (3 * count),
        out_specs=pl.BlockSpec(memory_space=pltpu.VMEM),
        scratch_shapes=[
            pltpu.VMEM((height, depth), BF16),
            pltpu.VMEM((depth, size), BF16),
            pltpu.SemaphoreType.DMA((3 * count,)),
        ],
        compiler_params=pltpu.CompilerParams(vmem_limit_bytes=VMEM_LIMIT),
        name=name,
    )(*lefts, *first, *second)


def across(block, axis, way):
    size = lax.axis_size(axis)
    route = [(i, i + way) for i in range(size) if 0 <= i + way < size]
    return lax.ppermute(block, axis, route)


def swap(block, axis, bits):
    size = lax.axis_size(axis)
    return lax.ppermute(block, axis, [(i, i ^ bits) for i in range(size)])


def after(value, *others):
    return lax.optimization_barrier((value,) + others)[0]


def spread(own):
    far = swap(own, "fsdp", 2)
    return [own, swap(own, "fsdp", 1), far, swap(far, "fsdp", 1)]


def in_order(pieces, me):
    odd, high = (me & 1) == 1, (me & 2) == 2
    a = jnp.where(odd, pieces[1], pieces[0])
    b = jnp.where(odd, pieces[0], pieces[1])
    c = jnp.where(odd, pieces[3], pieces[2])
    d = jnp.where(odd, pieces[2], pieces[3])
    low = [jnp.where(high, c, a), jnp.where(high, d, b)]
    return jnp.stack(low + [jnp.where(high, a, c), jnp.where(high, b, d)])


def line_sum(own, place):
    middle = (place == 1) | (place == 2)
    inward = lax.ppermute(own, "dp", [(0, 1), (3, 2)])
    half = (own.astype(F32) + inward.astype(F32)).astype(BF16)
    other = lax.ppermute(half, "dp", [(1, 2), (2, 1)])
    total = (half.astype(F32) + other.astype(F32)).astype(BF16)
    outward = lax.ppermute(total, "dp", [(1, 0), (2, 3)])
    return jnp.where(middle, total, outward).astype(F32)


def on_device(
    tokens,
    cotangent,
    lengths,
    norm_gain,
    in_weight,
    dt_weight,
    conv_weight,
    conv_bias,
    dt_bias,
    a_log,
    skip,
    gated_gain,
    out_weight,
):
    n = lax.axis_size("fsdp")
    square = n == 4 and lax.axis_size("dp") == 4
    section = lax.axis_index("section")
    me = lax.axis_index("fsdp")
    seq, width = tokens.shape[1], tokens.shape[2]
    proj = INNER + XBC
    smalls = (norm_gain, conv_weight, conv_bias, dt_bias, a_log, skip, gated_gain, dt_weight)
    packed = jnp.concatenate([s[0].reshape(-1) for s in smalls])
    if square:
        win = spread(in_weight[0])
        wout = spread(after(out_weight[0], win[2]))
        packed = in_order(spread(packed), me)
        order = jnp.stack([me, me ^ 1, me ^ 2, me ^ 3]).astype(jnp.int32)
    else:
        win = [lax.all_gather(in_weight[0], "fsdp", axis=0, tiled=True)]
        wout = [lax.all_gather(out_weight[0], "fsdp", axis=0, tiled=True)]
        packed = lax.all_gather(packed, "fsdp", axis=0)
        order = jnp.zeros((1,), jnp.int32)
    parts, place = [], 0
    for s in smalls:
        size = s.size
        parts.append(packed[:, place : place + size].reshape((n,) + s.shape[1:]))
        place += size

    def row(v, size=XBC):
        v = v.reshape(1, -1).astype(F32)
        return jnp.pad(v, ((0, 0), (0, size - v.shape[1])))

    conv_w = parts[1].transpose(1, 0, 2).reshape(CONV, XBC).astype(F32)
    sevens = jnp.concatenate([row(parts[3], LANES), row(parts[4], LANES), row(parts[5], LANES)], axis=1)
    pv = jnp.concatenate(
        [
            conv_w,
            row(parts[2]),
            row(parts[6]),
            row(parts[0]),
            row(sevens),
            row(jnp.repeat(parts[5].reshape(-1), HEAD_DIM)),
            jnp.zeros((7, XBC), F32),
        ]
    )
    wdt = jnp.pad(parts[7].reshape(width, HEADS), ((0, 0), (0, LANES - HEADS)))
    weights = (win, wout, wdt, pv)

    def meta_of(block):
        return jnp.concatenate(
            [
                jnp.stack([section.astype(jnp.int32), block.astype(jnp.int32), lengths[block, 0]]),
                order,
            ]
        )

    def keep(done, *keys):
        return {k: done[k] for k in done if k.startswith(keys)}

    at_zero = section == 0
    meta_p, meta_q = meta_of(section), meta_of(1 - section)
    first = layer_call(
        "first", 0, "s0", None, None, "s0", meta_p, tokens, None, None, None, weights, None, {}, True, False
    )
    arr_q = across(first["out"], "section", 1)
    second = layer_call(
        "second", 1, "all", None, "s1", "all", meta_q, tokens, cotangent, arr_q, None, weights, None,
        keep(first, "hu"), True, False,
    )
    arr_p = across(second["out"], "section", 1)
    arrg_p = across(second["dxb"], "section", -1)
    third = layer_call(
        "third", 0, "s1", "s0", "all", "all", meta_p, tokens, cotangent, arr_p, arrg_p, weights, first,
        {**keep(first, "out"), **keep(second, "hu")}, False, True,
    )
    arrg_q = across(third["dxb"], "section", -1)
    fourth = layer_call(
        "fourth", 1, None, "s0", "s0", "s0", meta_q, tokens, cotangent, None, arrg_q, weights, second,
        keep(second, "d", "small"), False, False,
    )
    live = jnp.arange(seq, dtype=jnp.int32) < meta_q[2]
    dout_q = jnp.where(at_zero, arrg_q, cotangent[0])
    dout_q = jnp.where(live[:, None], dout_q, jnp.zeros_like(dout_q))

    def by_block(p, q):
        return jnp.stack([jnp.where(at_zero, p, q), jnp.where(at_zero, q, p)])

    outputs = by_block(third["out"], second["out"])
    input_grads = by_block(third["dx"], fourth["dx"])
    small = third["small"] + fourth["small"]
    rows_in, rows_out = width // len(win), INNER // len(win)
    upper, lower = slice(0, rows_in), slice(rows_in, rows_in + rows_out)
    spans = (slice(0, width), slice(width, width + INNER), slice(width + INNER, width + proj + LANES))
    if square:
        hu = [third["hu0"]] + [swap(third[f"hu{k}"], "fsdp", k) for k in (1, 2, 3)]
        all_p = spread(third["all"])
        out_q = spread(dout_q)
        gate_q = spread(fourth["dgate"])
        side_q = spread(fourth["dside"])
        line = lax.axis_index("dp")
        grad_out = line_sum(weight_product("grad_out", hu, lower, all_p, spans[0], out_q), line)
        grad_gate = line_sum(weight_product("grad_gate", hu, upper, all_p, spans[1], gate_q), line)
        grad_side = line_sum(weight_product("grad_side", hu, upper, all_p, spans[2], side_q), line)
        for axis, bits in (("fsdp", 1), ("fsdp", 2), ("dp", 1), ("dp", 2)):
            small = small + swap(small, axis, bits)
    else:
        hu, all_p = [third["hu0"]], [third["all"]]
        grads = [
            weight_product("grad_out", hu, lower, all_p, spans[0], [dout_q]),
            weight_product("grad_gate", hu, upper, all_p, spans[1], [fourth["dgate"]]),
            weight_product("grad_side", hu, upper, all_p, spans[2], [fourth["dside"]]),
        ]
        grads = [lax.psum_scatter(g, "fsdp", scatter_dimension=0, tiled=True) for g in grads]
        grad_out, grad_gate, grad_side = [g.astype(F32) for g in lax.psum(grads, "dp")]
        small = lax.psum(small, ("dp", "fsdp"))

    def own(v):
        size = v.shape[-1] // n
        return lax.dynamic_slice_in_dim(v, me * size, size, axis=v.ndim - 1)

    return (
        outputs[None],
        input_grads[None],
        own(small[6:7, :width]),
        jnp.concatenate([grad_gate, grad_side[:, :XBC]], axis=1)[None],
        grad_side[None, :, XBC : XBC + HEADS],
        own(small[None, 0:CONV]),
        own(small[4:5]),
        own(small[7:8, 0:HEADS]),
        own(small[7:8, LANES : LANES + HEADS]),
        own(small[7:8, 2 * LANES : 2 * LANES + HEADS]),
        own(small[5:6, :INNER]),
        grad_out[None],
    )


def solution(mesh):
    in_specs = (
        P(None, ("dp", "fsdp"), None),
        P(None, ("dp", "fsdp"), None),
        P(None, ("dp", "fsdp")),
        P("section", "fsdp"),
        P("section", "fsdp", None),
        P("section", "fsdp", None),
        P("section", None, "fsdp"),
        P("section", "fsdp"),
        P("section", "fsdp"),
        P("section", "fsdp"),
        P("section", "fsdp"),
        P("section", "fsdp"),
        P("section", "fsdp", None),
    )
    out_specs = (
        P("section", None, ("dp", "fsdp"), None),
        P("section", None, ("dp", "fsdp"), None),
        P("section", "fsdp"),
        P("section", "fsdp", None),
        P("section", "fsdp", None),
        P("section", None, "fsdp"),
        P("section", "fsdp"),
        P("section", "fsdp"),
        P("section", "fsdp"),
        P("section", "fsdp"),
        P("section", "fsdp"),
        P("section", "fsdp", None),
    )
    return jax.shard_map(
        on_device, mesh=mesh, in_specs=in_specs, out_specs=out_specs, check_vma=False
    )
```

```python
import functools

import jax
import jax.numpy as jnp
from jax import lax
from jax.experimental import pallas as pl
from jax.experimental.pallas import tpu as pltpu
from jax.sharding import PartitionSpec as P

INNER = 1536
HEADS = 24
STATE = 128
HEAD_DIM = 64
CONV = 4
XBC = 1792
LANES = 128
TILE = 256
PAD = 8
CUT = 1024
WIN_CUTS = (slice(0, 512), slice(512, 1536), slice(1536, 2304), slice(2304, 3328))

EPS = 1e-05
F32 = jnp.float32
BF16 = jnp.bfloat16
ANY = pl.BlockSpec(memory_space=pl.ANY)
FAR = pl.BlockSpec(memory_space=pltpu.HBM)
VMEM_LIMIT = 60 * 1024 * 1024


def mm(a, b, contract=(1, 0), precision=None):
    dims = (((contract[0],), (contract[1],)), ((), ()))
    return lax.dot_general(a, b, dims, precision=precision, preferred_element_type=F32)


def sigmoid(v):
    return 1.0 / (1.0 + jnp.exp(-v))


def split_two(v):
    high = v.astype(BF16)
    return high, (v - high.astype(F32)).astype(BF16)


class Copies:
    def __init__(self, sems):
        self.sems = sems
        self.used = 0

    def make(self, source, target):
        copy = pltpu.make_async_copy(source, target, self.sems.at[self.used])
        self.used += 1
        return copy

    def start(self, source, target):
        copy = self.make(source, target)
        copy.start()
        return copy


def layer_kernel(cfg, *refs):
    r = dict(zip(cfg["names"], refs))
    n = cfg["pieces"]
    mode, block = cfg["mode"], cfg["block"]
    seq, width = cfg["seq"], cfg["width"]
    rows_in, rows_out = width // n, INNER // n
    order = [0]
    if n > 1:
        me = lax.axis_index("fsdp")
        order = [me ^ k for k in range(n)]
    length = r["lengths"][block]
    win, wout, wdt, pv = r["win_v"], r["wout_v"], r["wdt_v"], r["pv_v"]
    gate, xbc, y_s, raw_s, xs_s = r["gate_v"], r["xbc_v"], r["y_v"], r["raw_v"], r["xs_v"]
    inner_tiles = INNER // TILE
    conv_tiles = XBC // TILE
    pairs = INNER // LANES
    copies = Copies(r["sems"])

    def cols(k, size=TILE):
        return slice(k * size, (k + 1) * size)

    def body():
        copy_x = copies.start(r["tok"].at[block] if cfg["section"] == 0 else r["arr"], r["x_v"])
        copy_g, loads, wait_in, wait_out, params = None, [], [], [], []

        def load_in():
            for t in WIN_CUTS:
                waits = []
                for k in range(n):
                    row = pl.multiple_of(order[k] * rows_in, 16)
                    waits.append(copies.start(r[f"win{k}"].at[:, t], win.at[pl.ds(row, rows_in), t]))
                wait_in.append(waits)

        def load_out():
            for k in range(n):
                row = pl.multiple_of(order[k] * rows_out, 16)
                wait_out.append(copies.start(r[f"wout{k}"], wout.at[pl.ds(row, rows_out), :]))

        if mode != "out":
            params = [copies.start(r["pv"], pv), copies.start(r["wdt"], wdt)]
        if mode in ("both", "bwd", "gated", "scan"):
            copy_g = copies.start(r["cot"].at[block] if cfg["section"] == 1 else r["arrg"], r["g_v"])
        if mode == "bwd":
            load_out()
            loads = [
                copies.start(r["gate_i"], gate),
                copies.start(r["y_i"], y_s),
                copies.start(r["raw_i"], raw_s),
                copies.start(r["xs_i"], xs_s),
                copies.start(r["xbc_i"], xbc.at[PAD : PAD + seq, :]),
            ]
            load_in()
        elif mode == "gated":
            load_out()
            loads = [copies.start(r["gate_i"], gate), copies.start(r["y_i"], y_s)]
        elif mode == "scan":
            loads = [
                copies.start(r["raw_i"], raw_s),
                copies.start(r["xs_i"], xs_s),
                copies.start(r["dy_i"], r["a_v"]),
                copies.start(r["y_i"], y_s),
                copies.start(r["xbc_i"], xbc.at[PAD : PAD + seq, :]),
                copies.start(r["small_i"], r["small_v"]),
                copies.start(r["head_i"].at[:, width : width + INNER], r["dzx_v"].at[:, 0:INNER]),
            ]
            load_in()
        elif mode == "out":
            loads = [copies.start(r["u_i"], r["u_v"])]
            load_out()
        else:
            load_in()
            if mode != "start":
                load_out()

        def ready(waits):
            for copy in waits:
                copy.wait()
            waits.clear()

        below = lax.broadcasted_iota(jnp.int32, (seq, seq), 0) >= lax.broadcasted_iota(
            jnp.int32, (seq, seq), 1
        )
        row_id = lax.broadcasted_iota(jnp.int32, (seq, 1), 0)
        mask = jnp.where(row_id < length, 1.0, 0.0)
        lane = lax.broadcasted_iota(jnp.int32, (seq, LANES), 1)
        first_head = lane < HEAD_DIM
        xbc[0:PAD, :] = jnp.zeros((PAD, XBC), F32)
        copy_x.wait()
        ready(params)
        x = r["x_v"][...].astype(F32)
        scale = lax.rsqrt(jnp.mean(x * x, axis=-1, keepdims=True) + EPS)
        gain = pv[6:7, 0:width]
        outs = []

        def save(name, source):
            if name in r:
                outs.append(copies.start(source, r[name]))

        def finish_outs():
            for copy in outs:
                copy.wait()
            outs.clear()

        def conv_tile(k):
            t = cols(k)
            conv = pv[4:5, t]
            for tap in range(CONV):
                start = PAD - (CONV - 1) + tap
                conv = conv + xbc[start : start + seq, t] * pv[tap : tap + 1, t]
            return conv

        def steps(value):
            v = value + pv[7:8, 0:LANES]
            small = jnp.exp(-jnp.abs(v))
            dt = jnp.maximum(v, 0.0) + jnp.log1p(small)
            minus_a = -jnp.exp(pv[7:8, LANES : 2 * LANES])
            rate = dt * minus_a
            ones = jnp.where(below, 1.0, 0.0)
            cum = mm(ones, rate, precision=lax.Precision.HIGHEST)
            return v, dt, minus_a, rate, cum

        def forward():
            h = (x * scale * gain).astype(BF16)
            for waits, cut in zip(wait_in, WIN_CUTS):
                ready(waits)
                for start in range(cut.start, cut.stop, TILE):
                    value = mm(h, win[:, start : start + TILE])
                    if start < INNER:
                        gate[:, start : start + TILE] = value
                    else:
                        xbc[PAD : PAD + seq, start - INNER : start - INNER + TILE] = value
            raw = mm(h, wdt[...])
            raw_s[...] = raw
            save("gate_o", gate)
            save("xbc_o", xbc.at[PAD : PAD + seq, :])
            save("raw_o", raw_s)
            h_t = h.T
            r["ht_v"][...] = h_t
            for k in range(conv_tiles):
                conv = conv_tile(k)
                xs_s[:, cols(k)] = (conv * sigmoid(conv)).astype(BF16)
            save("xs_o", xs_s)
            _, dt, _, _, cum = steps(raw)
            cum_t, dt_t = cum.T, dt.T
            bmat = xs_s[:, INNER : INNER + STATE]
            cmat = xs_s[:, INNER + STATE : XBC]
            inner = mm(cmat, bmat, (1, 1))
            total = jnp.zeros((seq, LANES), F32)
            gated_v = r["a_v"]
            for p in range(pairs):
                t = cols(p, LANES)
                both = []
                for head in (2 * p, 2 * p + 1):
                    diff = cum[:, head : head + 1] - cum_t[head : head + 1, :]
                    decay = jnp.exp(jnp.where(below, diff, -1e30))
                    both.append((inner * decay * dt_t[head : head + 1, :]).astype(BF16))
                xp = xs_s[:, t]
                none = jnp.zeros_like(xp)
                wide = jnp.concatenate(
                    [jnp.where(first_head, xp, none), jnp.where(first_head, none, xp)], axis=0
                )
                y = mm(jnp.concatenate(both, axis=1), wide) + xp.astype(F32) * pv[8:9, t]
                y_s[:, t] = y
                z = gate[:, t]
                gated = y * (z * sigmoid(z))
                gated_v[:, t] = gated
                total = total + gated * gated
            save("y_o", y_s)
            back = lax.rsqrt(jnp.sum(total, axis=-1, keepdims=True) / INNER + EPS)
            for p in range(inner_tiles):
                t = cols(p)
                u = (gated_v[:, t] * back * pv[5:6, t]).astype(BF16)
                r["u_v"][:, t] = u
                r["ut_v"][t, :] = u.T
            save("u_o", r["u_v"])
            for k in range(n):
                a = pl.multiple_of(order[k] * rows_in, 16)
                b = pl.multiple_of(order[k] * rows_out, 16)
                target, below_it = r[f"hu{k % 2}_o"], (rows_in + rows_out) * (k // 2)
                place = slice(cfg["slot"] * seq, (cfg["slot"] + 1) * seq)
                outs.append(
                    copies.start(r["ht_v"].at[pl.ds(a, rows_in), :], target.at[below_it : below_it + rows_in, place])
                )
                outs.append(
                    copies.start(
                        r["ut_v"].at[pl.ds(b, rows_out), :],
                        target.at[below_it + rows_in : below_it + rows_in + rows_out, place],
                    )
                )

        def project():
            ready(wait_out)
            for k in range(width // TILE):
                t = cols(k)
                value = x[:, t] + mm(r["u_v"][...], wout[:, t])
                r["out_v"][:, t] = (value * mask).astype(BF16)
            save("out_o", r["out_v"])

        def backward():
            copy_g.wait()
            ready(loads)
            ready(wait_out)
            g = r["g_v"][...].astype(F32) * mask
            a_s, dact, dconv, dzx = r["a_v"], r["dact_v"], r["dconv_v"], r["dzx_v"]
            small = r["small_v"]
            if mode != "scan":
                gated_backward(g, a_s, dzx, small)
            if mode != "gated":
                scan_backward(g, a_s, dact, dconv, dzx, small)

        def gated_backward(g, a_s, dzx, small):
            r["dout_v"][...] = g.astype(BF16)
            target = r["all_o"] if "all_o" in r else r["head_o"]
            outs.append(copies.start(r["dout_v"], target.at[:, 0:width]))
            small[...] = jnp.zeros(small.shape, F32)
            total = jnp.zeros((seq, TILE), F32)
            mixed = jnp.zeros((seq, TILE), F32)
            for k in range(inner_tiles):
                t = cols(k)
                du = mm(r["dout_v"][...], wout[t, :], (1, 1))
                a_s[:, t] = du
                z = gate[:, t]
                gated = y_s[:, t] * (z * sigmoid(z))
                total = total + gated * gated
                mixed = mixed + du * pv[5:6, t] * gated
            back = lax.rsqrt(jnp.sum(total, axis=-1, keepdims=True) / INNER + EPS)
            pull = jnp.sum(mixed, axis=-1, keepdims=True) / INNER * back * back
            for k in range(inner_tiles):
                t = cols(k)
                z, y, du = gate[:, t], y_s[:, t], a_s[:, t]
                sig = sigmoid(z)
                act = z * sig
                gated = y * act
                small[5:6, t] = jnp.sum(du * gated * back, axis=0, keepdims=True)
                dgated = back * (du * pv[5:6, t] - gated * pull)
                a_s[:, t] = dgated * act
                dzx[:, t] = (dgated * y * (sig * (1.0 + z * (1.0 - sig)))).astype(BF16)
            target = r["all_o"] if "all_o" in r else r["head_o"]
            outs.append(copies.start(dzx.at[:, 0:INNER], target.at[:, width : width + INNER]))
            if mode == "gated":
                save("dy_o", a_s)
                save("small_o", small)

        def scan_backward(g, a_s, dact, dconv, dzx, small):
            dconv[seq : seq + PAD, :] = jnp.zeros((PAD, XBC), F32)
            v, dt, minus_a, rate, cum = steps(raw_s[...])
            cum_t, dt_t = cum.T, dt.T
            bmat = xs_s[:, INNER : INNER + STATE]
            cmat = xs_s[:, INNER + STATE : XBC]
            inner = mm(cmat, bmat, (1, 1))
            dinner = jnp.zeros((seq, seq), F32)
            dcum = jnp.zeros((seq, LANES), F32)
            dlast = jnp.zeros((seq, LANES), F32)
            dskip = jnp.zeros((PAD, LANES), F32)
            head_row = lax.broadcasted_iota(jnp.int32, (2 * LANES, LANES), 0)
            head_col = lax.broadcasted_iota(jnp.int32, (2 * LANES, LANES), 1)
            for p in range(pairs):
                t = cols(p, LANES)
                both, decays = [], []
                for head in (2 * p, 2 * p + 1):
                    diff = cum[:, head : head + 1] - cum_t[head : head + 1, :]
                    decay = jnp.exp(jnp.where(below, diff, -1e30))
                    both.append((inner * decay * dt_t[head : head + 1, :]).astype(BF16))
                    decays.append(decay * dt_t[head : head + 1, :])
                scores = jnp.concatenate(both, axis=1)
                xp = xs_s[:, t]
                none = jnp.zeros_like(xp)
                wide = jnp.concatenate(
                    [jnp.where(first_head, xp, none), jnp.where(first_head, none, xp)], axis=0
                )
                dy = a_s[:, t]
                dy_low = dy.astype(BF16)
                dscores = mm(dy_low, wide, (1, 1))
                dinner = dinner + dscores[:, 0:seq] * decays[0] + dscores[:, seq:] * decays[1]
                spread = mm(scores, dy_low, (0, 0))
                dxs = jnp.where(first_head, spread[0:seq], spread[seq:])
                xf = xp.astype(F32)
                skip = pv[8:9, t]
                dact[:, t] = dy * skip + dxs
                own = jnp.where(head_col == 2 * p + (head_row % LANES) // HEAD_DIM, 1.0, 0.0).astype(BF16)
                left = xf * dxs
                dlast = dlast + mm(jnp.concatenate(split_two(left), axis=1), own)
                gap = dy_low.astype(F32) * (y_s[:, t] - skip * xf) - left
                dcum = dcum + mm(jnp.concatenate(split_two(gap), axis=1), own)
                by_lane = jnp.sum(dy * xf, axis=0, keepdims=True)
                by_lane = jnp.broadcast_to(by_lane, (PAD, LANES))
                dskip = dskip + mm(jnp.concatenate(split_two(by_lane), axis=1), own)
            above = jnp.where(
                lax.broadcasted_iota(jnp.int32, (seq, seq), 0)
                <= lax.broadcasted_iota(jnp.int32, (seq, seq), 1),
                1.0,
                0.0,
            )
            drate = mm(above, dcum, precision=lax.Precision.HIGHEST)
            sig = sigmoid(v)
            ratio = jnp.where(v < -15.0, 1.0, sig / jnp.maximum(dt, 1e-30))
            draw = drate * minus_a * sig + dlast * ratio
            draw_low = draw.astype(BF16)
            dzx[:, INNER + XBC : INNER + XBC + LANES] = draw_low
            small[7:8, 0:LANES] = jnp.sum(draw, axis=0, keepdims=True)
            small[7:8, LANES : 2 * LANES] = jnp.sum(drate * rate, axis=0, keepdims=True)
            small[7:8, 2 * LANES : 3 * LANES] = dskip[0:1, :]
            dinner_low = dinner.astype(BF16)
            dact[:, INNER : INNER + STATE] = mm(dinner_low, cmat, (0, 0))
            dact[:, INNER + STATE : XBC] = mm(dinner_low, bmat)
            for k in range(conv_tiles):
                t = cols(k)
                conv = conv_tile(k)
                sig = sigmoid(conv)
                grad = dact[:, t] * (sig * (1.0 + conv * (1.0 - sig)))
                dconv[0:seq, t] = grad
                small[4:5, t] = jnp.sum(grad, axis=0, keepdims=True)
                dxbc = jnp.zeros((seq, TILE), F32)
                for tap in range(CONV):
                    start = PAD - (CONV - 1) + tap
                    small[tap : tap + 1, t] = jnp.sum(
                        grad * xbc[start : start + seq, t], axis=0, keepdims=True
                    )
                    ahead = CONV - 1 - tap
                    dxbc = dxbc + dconv[ahead : ahead + seq, t] * pv[tap : tap + 1, t]
                dzx[:, INNER + k * TILE : INNER + (k + 1) * TILE] = dxbc.astype(BF16)
            if "all_o" in r:
                target = r["all_o"].at[:, width + INNER : width + INNER + XBC + LANES]
                outs.append(copies.start(dzx.at[:, INNER : INNER + XBC + LANES], target))
            else:
                outs.append(copies.start(dzx.at[:, INNER : INNER + XBC + LANES], r["dside_o"]))
            dh = r["dh_v"]
            for waits in wait_in:
                ready(waits)
            for k in range(width // TILE):
                t = cols(k)
                dh[:, t] = mm(dzx[:, 0 : INNER + XBC], win[t, :], (1, 1)) + mm(draw_low, wdt[t, :], (1, 1))
            product = dh[...] * gain
            pulled = jnp.mean(product * x, axis=-1, keepdims=True) * scale * scale
            dx = g + scale * (product - x * pulled)
            small[6:7, 0:width] = jnp.sum(dh[...] * x * scale, axis=0, keepdims=True)
            dh[...] = dx
            r["dxb_v"][...] = dx.astype(BF16)
            if "dxb_o" in r:
                save("dxb_o", r["dxb_v"])
            save("dx_o", dh)
            save("small_o", small)

        if mode in ("start", "fwd", "both"):
            forward()
        if mode == "out":
            ready(loads)
        if mode in ("out", "fwd", "both"):
            project()
        if mode in ("both", "bwd", "gated", "scan"):
            backward()
        finish_outs()

    pl.when(lax.axis_index("section") == cfg["section"])(body)


RESIDUALS = ("gate", "xbc", "y", "raw", "xs")
COST = dict(start=8000, out=2000, fwd=9000, both=18000, bwd=13000, gated=5000, scan=10000)
RESIDUALS_USED = dict(
    bwd=RESIDUALS, gated=("gate", "y"), scan=("raw", "xs", "dy", "y", "xbc", "small", "head"), out=("u",)
)


def layer_call(
    name,
    section,
    slot,
    block,
    mode,
    args,
    weights,
    residual=None,
    kept=None,
    save=False,
    one_array=False,
    ahead=(),
):
    win, wout, wdt, pv = weights
    kept = kept or {}
    n = args["pieces"]
    seq, width = args["tok"].shape[1], args["tok"].shape[2]
    rows = width // n + INNER // n
    proj = INNER + XBC
    shapes = dict(
        gate=((seq, INNER), F32),
        xbc=((seq, XBC), F32),
        y=((seq, INNER), F32),
        raw=((seq, LANES), F32),
        xs=((seq, XBC), BF16),
        out=((seq, width), BF16),
        u=((seq, INNER), BF16),
        dy=((seq, INNER), F32),
        all=((seq, width + proj + LANES), BF16),
        head=((seq, width + INNER), BF16),
        dside=((seq, XBC + LANES), BF16),
        dx=((seq, width), F32),
        dxb=((seq, width), BF16),
        small=((8, XBC), F32),
    )
    for k in range(min(n, 2)):
        shapes[f"hu{k}"] = ((rows * (2 if n > 1 else 1), 2 * seq), BF16)
    inputs = [("lengths", args["lengths"], pl.BlockSpec(memory_space=pltpu.SMEM))]
    inputs.append(("tok", args["tok"], FAR) if section == 0 else ("arr", args["arr"], ANY))
    if mode in ("both", "bwd", "gated", "scan"):
        inputs.append(("cot", args["cot"], FAR) if section == 1 else ("arrg", args["arrg"], ANY))
    if mode not in ("out", "gated"):
        inputs += [(f"win{k}", w, FAR) for k, w in enumerate(win)]
    if mode != "out":
        inputs += [("wdt", wdt, FAR), ("pv", pv, FAR)]
    if mode not in ("start", "scan"):
        inputs += [(f"wout{k}", w, FAR) for k, w in enumerate(wout)]
    inputs += [(f"{k}_i", residual[k], FAR) for k in RESIDUALS_USED.get(mode, ())]
    inputs += [(f"ahead{k}", value, FAR) for k, value in enumerate(ahead)]
    outputs = []
    if mode in ("start", "fwd", "both"):
        outputs += [f"hu{k}" for k in range(min(n, 2))]
        if save:
            outputs += list(RESIDUALS)
    if mode == "start":
        outputs.append("u")
    if mode in ("out", "fwd", "both"):
        outputs.append("out")
    if mode in ("both", "bwd"):
        outputs += ["all"] if one_array else ["head", "dside"]
        outputs += ["dx", "small"]
        if section == 1:
            outputs.append("dxb")
    if mode == "gated":
        outputs += ["head", "dy", "small"]
    if mode == "scan":
        outputs += ["dside", "dx", "small"]
    aliases = {}
    for place, key in enumerate(outputs):
        if key in kept:
            aliases[len(inputs)] = place
            inputs.append((f"{key}_k", kept[key], FAR))
    scratch = dict(
        x_v=((seq, width), BF16),
        g_v=((seq, width), BF16),
        dout_v=((seq, width), BF16),
        out_v=((seq, width), BF16),
        dxb_v=((seq, width), BF16),
        win_v=((width, proj), BF16),
        wout_v=((INNER, width), BF16),
        wdt_v=((width, LANES), BF16),
        pv_v=(pv.shape, F32),
        gate_v=((seq, INNER), F32),
        xbc_v=((seq + PAD, XBC), F32),
        y_v=((seq, INNER), F32),
        raw_v=((seq, LANES), F32),
        xs_v=((seq, XBC), BF16),
        ht_v=((width, seq), BF16),
        u_v=((seq, INNER), BF16),
        ut_v=((INNER, seq), BF16),
        a_v=((seq, INNER), F32),
        dact_v=((seq, XBC), F32),
        dconv_v=((seq + PAD, XBC), F32),
        dzx_v=((seq, proj + LANES), BF16),
        dh_v=((seq, width), F32),
        small_v=((8, XBC), F32),
    )
    names = [k for k, _, _ in inputs] + [f"{k}_o" for k in outputs] + list(scratch) + ["sems"]
    cfg = dict(
        names=names, pieces=n, section=section, slot=slot, block=block, mode=mode, seq=seq, width=width
    )
    results = pl.pallas_call(
        functools.partial(layer_kernel, cfg),
        out_shape=[jax.ShapeDtypeStruct(*shapes[k]) for k in outputs],
        in_specs=[spec for _, _, spec in inputs],
        out_specs=[FAR for _ in outputs],
        scratch_shapes=[pltpu.VMEM(*v) for v in scratch.values()]
        + [pltpu.SemaphoreType.DMA((12 * n + 32,))],
        input_output_aliases=aliases,
        cost_estimate=pl.CostEstimate(flops=COST[mode] * 10**6, bytes_accessed=10**6, transcendentals=0),
        compiler_params=pltpu.CompilerParams(vmem_limit_bytes=VMEM_LIMIT),
        name=name,
    )(*[value for _, value, _ in inputs])
    return dict(zip(outputs, results))


def product_kernel(rows, places, parts, count, extra, *refs):
    lefts, first, second = refs[:count], refs[count : 2 * count], refs[2 * count : 3 * count]
    smalls = refs[3 * count : 3 * count + extra]
    outs, (left_v, right_v, small_v, sems) = refs[-4 - len(parts) : -4], refs[-4:]
    seq = first[0].shape[0]
    copies = Copies(sems)
    waits = []
    for k in range(count):
        start = 2 * k * seq
        waits.append(copies.start(lefts[k].at[rows, :], left_v.at[:, start : start + 2 * seq]))
        for slot, side in enumerate((first[k], second[k])):
            at = start + slot * seq
            waits.append(copies.start(side.at[:, places[slot]], right_v.at[at : at + seq, :]))
    for k in range(extra):
        waits.append(copies.start(smalls[k], small_v.at[k]))
    for copy in waits:
        copy.wait()
    if extra:
        total = small_v[0]
        for k in range(1, extra):
            total = total + small_v[k]
        half = total.shape[1] // 2
        total = jnp.concatenate([total[:, :half], total[:, half:]], axis=0)
        for out in outs[-2:]:
            out[out.shape[0] - 16 :, :] = total.astype(out.dtype)
    for out, (height, above, at, size) in zip(outs, parts):
        for k in range(0, size, TILE):
            end = min(k + TILE, size)
            value = mm(left_v[above : above + height, :], right_v[:, at + k : at + end])
            out[0:height, k:end] = value.astype(out.dtype)


def weight_product(name, lefts, rows, first, second, places, parts, ahead=(), smalls=()):
    count = len(lefts)
    depth = 2 * count * first[0].shape[0]
    tall, wide = rows.stop - rows.start, places[0].stop - places[0].start
    shapes = [(part[0], part[3]) for part in parts]
    if smalls:
        shapes[-2:] = [(height + 16, size) for height, size in shapes[-2:]]
    return pl.pallas_call(
        functools.partial(product_kernel, rows, places, parts, count, len(smalls)),
        out_shape=[jax.ShapeDtypeStruct(shape, BF16) for shape in shapes],
        in_specs=[FAR] * (3 * count + len(smalls) + len(ahead)),
        out_specs=[pl.BlockSpec(memory_space=pltpu.VMEM) for _ in shapes],
        scratch_shapes=[
            pltpu.VMEM((tall, depth), BF16),
            pltpu.VMEM((depth, wide), BF16),
            pltpu.VMEM((2, 8, XBC), F32),
            pltpu.SemaphoreType.DMA((3 * count + 2,)),
        ],
        cost_estimate=pl.CostEstimate(flops=10**6, bytes_accessed=10**6, transcendentals=0),
        compiler_params=pltpu.CompilerParams(vmem_limit_bytes=VMEM_LIMIT),
        name=name,
    )(*lefts, *first, *second, *smalls, *ahead)


def across(block, axis, way):
    size = lax.axis_size(axis)
    route = [(i, i + way) for i in range(size) if 0 <= i + way < size]
    return lax.ppermute(block, axis, route)


def swap(block, axis, bits):
    size = lax.axis_size(axis)
    return lax.ppermute(block, axis, [(i, i ^ bits) for i in range(size)])


def after(value, *others):
    return lax.optimization_barrier((value,) + others)[0]


def spread(own):
    far = swap(own, "fsdp", 2)
    return [own, swap(own, "fsdp", 1), far, swap(far, "fsdp", 1)]


def beside(own):
    return [own, swap(own, "fsdp", 1)]


def in_order(pieces, me):
    odd, high = (me & 1) == 1, (me & 2) == 2
    a = jnp.where(odd, pieces[1], pieces[0])
    b = jnp.where(odd, pieces[0], pieces[1])
    c = jnp.where(odd, pieces[3], pieces[2])
    d = jnp.where(odd, pieces[2], pieces[3])
    low = [jnp.where(high, c, a), jnp.where(high, d, b)]
    return jnp.stack(low + [jnp.where(high, a, c), jnp.where(high, b, d)])


def group_sums(own_parts, far_parts, place):
    middle = (place == 1) | (place == 2)
    count = len(own_parts)
    arrived, halves, totals, outwards = [], [], [], []

    def done(values, k):
        return [values[k]] if 0 <= k < len(values) else []

    for step in range(count + 2):
        if step < count:
            far = after(far_parts[step], *done(arrived, step - 2), *done(halves, step - 3))
            arrived.append(swap(far, "fsdp", 2))
        k = step - 1
        if 0 <= k < count:
            own = (own_parts[k].astype(F32) + arrived[k].astype(F32)).astype(BF16)
            own = after(own, *done(halves, k - 2))
            inward = lax.ppermute(own, "dp", [(0, 1), (3, 2)])
            inward = after(inward, *done(arrived, k + 1), *done(totals, k - 2))
            halves.append((own.astype(F32) + inward.astype(F32)).astype(BF16))
        k = step - 2
        if 0 <= k < count:
            other = lax.ppermute(halves[k], "dp", [(1, 2), (2, 1)])
            other = after(other, *done(halves, k + 1), *done(outwards, k - 2))
            totals.append((halves[k].astype(F32) + other.astype(F32)).astype(BF16))
            outwards.append(lax.ppermute(totals[k], "dp", [(1, 0), (2, 3)]))
    return [jnp.where(middle, t, o).astype(F32) for t, o in zip(totals, outwards)]


def on_device(
    tokens,
    cotangent,
    lengths,
    norm_gain,
    in_weight,
    dt_weight,
    conv_weight,
    conv_bias,
    dt_bias,
    a_log,
    skip,
    gated_gain,
    out_weight,
):
    n = lax.axis_size("fsdp")
    square = n == 4 and lax.axis_size("dp") == 4
    section = lax.axis_index("section")
    me = lax.axis_index("fsdp")
    seq, width = tokens.shape[1], tokens.shape[2]
    proj = INNER + XBC
    smalls = (norm_gain, conv_weight, conv_bias, dt_bias, a_log, skip, gated_gain, dt_weight)
    packed = jnp.concatenate([s[0].reshape(-1) for s in smalls])
    if square:
        win = spread(in_weight[0])
        lengths, packed = lax.optimization_barrier((lengths.reshape(-1), packed))
        far_out = swap(after(out_weight[0], packed), "fsdp", 2)
        packed = in_order(spread(packed), me)
    else:
        win = [lax.all_gather(in_weight[0], "fsdp", axis=0, tiled=True)]
        wout = [lax.all_gather(out_weight[0], "fsdp", axis=0, tiled=True)]
        packed = lax.all_gather(packed, "fsdp", axis=0)
        lengths = lengths.reshape(-1)
    parts, place = [], 0
    for s in smalls:
        size = s.size
        parts.append(packed[:, place : place + size].reshape((n,) + s.shape[1:]))
        place += size

    def row(v, size=XBC):
        v = v.reshape(1, -1).astype(F32)
        return jnp.pad(v, ((0, 0), (0, size - v.shape[1])))

    conv_w = parts[1].transpose(1, 0, 2).reshape(CONV, XBC).astype(F32)
    sevens = jnp.concatenate([row(parts[3], LANES), row(parts[4], LANES), row(parts[5], LANES)], axis=1)
    pv = jnp.concatenate(
        [
            conv_w,
            row(parts[2]),
            row(parts[6]),
            row(parts[0]),
            row(sevens),
            row(jnp.repeat(parts[5].reshape(-1), HEAD_DIM)),
            jnp.zeros((7, XBC), F32),
        ]
    )
    wdt = jnp.pad(parts[7].reshape(width, HEADS), ((0, 0), (0, LANES - HEADS)))

    def keep(done, *keys):
        return {k: done[k] for k in done if k.startswith(keys)}

    at_zero = section == 0
    pieces = n if square else 1
    args = dict(tok=tokens, cot=cotangent, lengths=lengths, pieces=pieces)
    fwd_p = layer_call("start_p", 0, 0, 0, "start", args, (win, [], wdt, pv), save=True)
    if square:
        last = swap(after(far_out, fwd_p["u"]), "fsdp", 1)
        wout = [out_weight[0], swap(out_weight[0], "fsdp", 1), far_out, last]
    weights = (win, wout, wdt, pv)
    fwd_p.update(layer_call("out_p", 0, 0, 0, "out", args, weights, fwd_p))
    args["arr"] = across(fwd_p["out"], "section", 1)
    fwd_q = layer_call("fwd_q", 0, 1, 1, "fwd", args, weights, kept=keep(fwd_p, "hu"), save=True)
    arr_p = across(fwd_q["out"], "section", 1)
    both_q = layer_call("both_q", 1, 1, 0, "both", args, weights, kept=keep(fwd_q, "hu"))
    args["arrg"] = across(both_q["dxb"], "section", -1)
    args["arr"] = arr_p
    both_p = layer_call("both_p", 1, 0, 1, "both", args, weights, kept=keep(both_q, "hu"), one_array=True)
    arrg_q = across(both_p["dxb"], "section", -1)
    bwd_p = layer_call(
        "bwd_p", 0, 0, 0, "bwd", args, weights, fwd_p, keep(both_p, "all", "dx", "small"),
        one_array=True,
    )
    args["arrg"] = arrg_q
    gated_q = layer_call(
        "gated_q", 0, 1, 1, "gated", args, weights, fwd_q, keep(both_q, "head"),
        ahead=[bwd_p["dx"]],
    )
    rows_in, rows_out = width // pieces, INNER // pieces
    height = rows_in + rows_out
    hu, all_p, head_q = [both_p["hu0"]], [bwd_p["all"]], [gated_q["head"]]
    bases = (0,)
    if square:
        hu, all_p, head_q = hu + [swap(both_p["hu1"], "fsdp", 1)], beside(all_p[0]), beside(head_q[0])
        bases = (0, height)

    def parts_of(*parts):
        return tuple((size, base + row, at, wide) for size, row, at, wide in parts for base in bases)

    places = (slice(0, width + INNER),) * 2
    head_parts = (
        (rows_out // 2, rows_in, 0, width),
        (rows_out // 2, rows_in + rows_out // 2, 0, width),
        (rows_in, 0, width, INNER // 2),
        (rows_in, 0, width + INNER // 2, INNER // 2),
    )
    if not square:
        head_parts = ((rows_out, rows_in, 0, width), *head_parts[2:])
    parts = parts_of(*head_parts)
    grads = weight_product("grad_head", hu, slice(0, height * len(bases)), all_p, head_q, places, parts)
    scan_q = layer_call(
        "scan_q", 0, 1, 1, "scan", args, weights, {**fwd_q, **gated_q},
        keep(both_q, "dside", "dx", "small"), ahead=grads[:1],
    )
    small = bwd_p["small"] + scan_q["small"]
    side_q, smalls, ahead = [scan_q["dside"]], [], ()
    if square:
        side_q, smalls = beside(side_q[0]), beside(small)
    places = (slice(width + INNER, width + proj + LANES), slice(0, XBC + LANES))
    parts = parts_of((rows_in, 0, 0, CUT), (rows_in, 0, CUT, XBC + LANES - CUT))
    grads += weight_product(
        "grad_side", hu, slice(0, height * len(bases)), all_p, side_q, places, parts, (), smalls
    )

    def by_block(p, q):
        return jnp.stack([jnp.where(at_zero, p, q), jnp.where(at_zero, q, p)])

    outputs = by_block(
        jnp.where(at_zero, fwd_p["out"], both_p["out"]), jnp.where(at_zero, fwd_q["out"], both_q["out"])
    )
    input_grads = by_block(bwd_p["dx"], scan_q["dx"])
    if square:
        line = lax.axis_index("dp")
        grads = group_sums(grads[0::2], grads[1::2], line)
        small = grads[-1][rows_in:]
        small = jnp.concatenate([small[:8], small[8:]], axis=1)
    else:
        grads = [lax.psum_scatter(g, "fsdp", scatter_dimension=0, tiled=True) for g in grads]
        grads = [g.astype(F32) for g in lax.psum(grads, "dp")]
        small = lax.psum(small, ("dp", "fsdp"))
    *grad_out, gate_low, gate_high, grad_near, grad_rest = grads
    rows_own = width // n

    def own(v):
        size = v.shape[-1] // n
        return lax.dynamic_slice_in_dim(v, me * size, size, axis=v.ndim - 1)

    return (
        outputs[None],
        input_grads[None],
        own(small[6:7, :width]),
        jnp.concatenate([gate_low, gate_high, grad_near, grad_rest[:rows_own, : XBC - CUT]], axis=1)[None],
        grad_rest[None, :rows_own, XBC - CUT : XBC - CUT + HEADS],
        own(small[None, 0:CONV]),
        own(small[4:5]),
        own(small[7:8, 0:HEADS]),
        own(small[7:8, LANES : LANES + HEADS]),
        own(small[7:8, 2 * LANES : 2 * LANES + HEADS]),
        own(small[5:6, :INNER]),
        jnp.concatenate(grad_out)[None],
    )


def solution(mesh):
    in_specs = (
        P(None, ("dp", "fsdp"), None),
        P(None, ("dp", "fsdp"), None),
        P(None, ("dp", "fsdp")),
        P("section", "fsdp"),
        P("section", "fsdp", None),
        P("section", "fsdp", None),
        P("section", None, "fsdp"),
        P("section", "fsdp"),
        P("section", "fsdp"),
        P("section", "fsdp"),
        P("section", "fsdp"),
        P("section", "fsdp"),
        P("section", "fsdp", None),
    )
    out_specs = (
        P("section", None, ("dp", "fsdp"), None),
        P("section", None, ("dp", "fsdp"), None),
        P("section", "fsdp"),
        P("section", "fsdp", None),
        P("section", "fsdp", None),
        P("section", None, "fsdp"),
        P("section", "fsdp"),
        P("section", "fsdp"),
        P("section", "fsdp"),
        P("section", "fsdp"),
        P("section", "fsdp"),
        P("section", "fsdp", None),
    )
    return jax.shard_map(
        on_device, mesh=mesh, in_specs=in_specs, out_specs=out_specs, check_vma=False
    )
```

```python
import functools

import jax
import jax.numpy as jnp
from jax import lax
from jax.experimental import pallas as pl
from jax.experimental.pallas import tpu as pltpu
from jax.sharding import PartitionSpec as P

INNER = 1536
HEADS = 24
STATE = 128
HEAD_DIM = 64
CONV = 4
XBC = 1792
LANES = 128
TILE = 256
PAD = 8
CUT = 1024
WIN_CUTS = (slice(0, 512), slice(512, 1536), slice(1536, 3328))

EPS = 1e-05
F32 = jnp.float32
BF16 = jnp.bfloat16
ANY = pl.BlockSpec(memory_space=pl.ANY)
FAR = pl.BlockSpec(memory_space=pltpu.HBM)
VMEM_LIMIT = 60 * 1024 * 1024


def mm(a, b, contract=(1, 0), precision=None):
    dims = (((contract[0],), (contract[1],)), ((), ()))
    return lax.dot_general(a, b, dims, precision=precision, preferred_element_type=F32)


def sigmoid(v):
    return 1.0 / (1.0 + jnp.exp(-v))


def split_two(v):
    high = v.astype(BF16)
    return high, (v - high.astype(F32)).astype(BF16)


class Copies:
    def __init__(self, sems):
        self.sems = sems
        self.used = 0

    def make(self, source, target):
        copy = pltpu.make_async_copy(source, target, self.sems.at[self.used])
        self.used += 1
        return copy

    def start(self, source, target):
        copy = self.make(source, target)
        copy.start()
        return copy


def layer_kernel(cfg, *refs):
    r = dict(zip(cfg["names"], refs))
    n = cfg["pieces"]
    mode, block = cfg["mode"], cfg["block"]
    seq, width = cfg["seq"], cfg["width"]
    rows_in, rows_out = width // n, INNER // n
    order = [0]
    if n > 1:
        me = lax.axis_index("fsdp")
        order = [me ^ k for k in range(n)]
        pair = lax.axis_index("dp") & 1
    length = r["lengths"][block]
    in_places = [(order[k] * rows_in, rows_in) for k in range(min(n, 2))]
    out_places = [(order[k] * rows_out, rows_out) for k in range(min(n, 2))]
    if n > 1:
        for k in (2, 3):
            for part in range(4):
                number = 2 * (pair ^ (part & 1)) + part // 2
                in_places.append((order[k] * rows_in + number * (rows_in // 4), rows_in // 4))
            for part in range(2):
                out_places.append((order[k] * rows_out + (pair ^ part) * (rows_out // 2), rows_out // 2))
    win, wout, wdt, pv = r["win_v"], r["wout_v"], r["wdt_v"], r["pv_v"]
    gate, xbc, y_s, raw_s, xs_s = r["gate_v"], r["xbc_v"], r["y_v"], r["raw_v"], r["xs_v"]
    inner_tiles = INNER // TILE
    conv_tiles = XBC // TILE
    pairs = INNER // LANES
    copies = Copies(r["sems"])

    def cols(k, size=TILE):
        return slice(k * size, (k + 1) * size)

    def body():
        copy_x = copies.start(r["tok"].at[block] if cfg["section"] == 0 else r["arr"], r["x_v"])
        copy_g, loads, wait_in, wait_out, params = None, [], [], [], []

        def load_in():
            for t in WIN_CUTS:
                waits = []
                for k, (row, rows) in enumerate(in_places):
                    row = pl.multiple_of(row, 16)
                    waits.append(copies.start(r[f"win{k}"].at[:, t], win.at[pl.ds(row, rows), t]))
                wait_in.append(waits)

        def load_out():
            for k, (row, rows) in enumerate(out_places):
                row = pl.multiple_of(row, 16)
                wait_out.append(copies.start(r[f"wout{k}"], wout.at[pl.ds(row, rows), :]))

        if mode != "out":
            params = [copies.start(r["pv"], pv), copies.start(r["wdt"], wdt)]
        if mode in ("both", "bwd", "gated", "scan"):
            copy_g = copies.start(r["cot"].at[block] if cfg["section"] == 1 else r["arrg"], r["g_v"])
        if mode == "bwd":
            load_out()
            loads = [
                copies.start(r["gate_i"], gate),
                copies.start(r["y_i"], y_s),
                copies.start(r["raw_i"], raw_s),
                copies.start(r["xs_i"], xs_s),
                copies.start(r["xbc_i"], xbc.at[PAD : PAD + seq, :]),
            ]
            load_in()
        elif mode == "gated":
            load_out()
            loads = [copies.start(r["gate_i"], gate), copies.start(r["y_i"], y_s)]
        elif mode == "scan":
            loads = [
                copies.start(r["raw_i"], raw_s),
                copies.start(r["xs_i"], xs_s),
                copies.start(r["dy_i"], r["a_v"]),
                copies.start(r["y_i"], y_s),
                copies.start(r["xbc_i"], xbc.at[PAD : PAD + seq, :]),
                copies.start(r["small_i"], r["small_v"]),
                copies.start(r["head_i"].at[:, width : width + INNER], r["dzx_v"].at[:, 0:INNER]),
            ]
            load_in()
        elif mode == "out":
            loads = [copies.start(r["u_i"], r["u_v"])]
            load_out()
        else:
            load_in()
            if mode != "start":
                load_out()

        def ready(waits):
            for copy in waits:
                copy.wait()
            waits.clear()

        below = lax.broadcasted_iota(jnp.int32, (seq, seq), 0) >= lax.broadcasted_iota(
            jnp.int32, (seq, seq), 1
        )
        row_id = lax.broadcasted_iota(jnp.int32, (seq, 1), 0)
        mask = jnp.where(row_id < length, 1.0, 0.0)
        lane = lax.broadcasted_iota(jnp.int32, (seq, LANES), 1)
        first_head = lane < HEAD_DIM
        xbc[0:PAD, :] = jnp.zeros((PAD, XBC), F32)
        copy_x.wait()
        ready(params)
        x = r["x_v"][...].astype(F32)
        scale = lax.rsqrt(jnp.mean(x * x, axis=-1, keepdims=True) + EPS)
        gain = pv[6:7, 0:width]
        outs = []

        def save(name, source):
            if name in r:
                outs.append(copies.start(source, r[name]))

        def finish_outs():
            for copy in outs:
                copy.wait()
            outs.clear()

        def conv_tile(k):
            t = cols(k)
            conv = pv[4:5, t]
            for tap in range(CONV):
                start = PAD - (CONV - 1) + tap
                conv = conv + xbc[start : start + seq, t] * pv[tap : tap + 1, t]
            return conv

        def steps(value):
            v = value + pv[7:8, 0:LANES]
            small = jnp.exp(-jnp.abs(v))
            dt = jnp.maximum(v, 0.0) + jnp.log1p(small)
            minus_a = -jnp.exp(pv[7:8, LANES : 2 * LANES])
            rate = dt * minus_a
            ones = jnp.where(below, 1.0, 0.0)
            cum = mm(ones, rate, precision=lax.Precision.HIGHEST)
            return v, dt, minus_a, rate, cum

        def forward():
            h = (x * scale * gain).astype(BF16)
            for waits, cut in zip(wait_in, WIN_CUTS):
                ready(waits)
                for start in range(cut.start, cut.stop, TILE):
                    value = mm(h, win[:, start : start + TILE])
                    if start < INNER:
                        gate[:, start : start + TILE] = value
                    else:
                        xbc[PAD : PAD + seq, start - INNER : start - INNER + TILE] = value
            raw = mm(h, wdt[...])
            raw_s[...] = raw
            save("gate_o", gate)
            save("xbc_o", xbc.at[PAD : PAD + seq, :])
            save("raw_o", raw_s)
            h_t = h.T
            r["ht_v"][...] = h_t
            for k in range(conv_tiles):
                conv = conv_tile(k)
                xs_s[:, cols(k)] = (conv * sigmoid(conv)).astype(BF16)
            save("xs_o", xs_s)
            _, dt, _, _, cum = steps(raw)
            cum_t, dt_t = cum.T, dt.T
            bmat = xs_s[:, INNER : INNER + STATE]
            cmat = xs_s[:, INNER + STATE : XBC]
            inner = mm(cmat, bmat, (1, 1))
            total = jnp.zeros((seq, LANES), F32)
            gated_v = r["a_v"]
            for p in range(pairs):
                t = cols(p, LANES)
                both = []
                for head in (2 * p, 2 * p + 1):
                    diff = cum[:, head : head + 1] - cum_t[head : head + 1, :]
                    decay = jnp.exp(jnp.where(below, diff, -1e30))
                    both.append((inner * decay * dt_t[head : head + 1, :]).astype(BF16))
                xp = xs_s[:, t]
                none = jnp.zeros_like(xp)
                wide = jnp.concatenate(
                    [jnp.where(first_head, xp, none), jnp.where(first_head, none, xp)], axis=0
                )
                y = mm(jnp.concatenate(both, axis=1), wide) + xp.astype(F32) * pv[8:9, t]
                y_s[:, t] = y
                z = gate[:, t]
                gated = y * (z * sigmoid(z))
                gated_v[:, t] = gated
                total = total + gated * gated
            save("y_o", y_s)
            back = lax.rsqrt(jnp.sum(total, axis=-1, keepdims=True) / INNER + EPS)
            for p in range(inner_tiles):
                t = cols(p)
                u = (gated_v[:, t] * back * pv[5:6, t]).astype(BF16)
                r["u_v"][:, t] = u
                r["ut_v"][t, :] = u.T
            save("u_o", r["u_v"])
            for k in range(n):
                a = pl.multiple_of(order[k] * rows_in, 16)
                b = pl.multiple_of(order[k] * rows_out, 16)
                target, below_it = r[f"hu{k % 2}_o"], (rows_in + rows_out) * (k // 2)
                place = slice(cfg["slot"] * seq, (cfg["slot"] + 1) * seq)
                outs.append(
                    copies.start(r["ht_v"].at[pl.ds(a, rows_in), :], target.at[below_it : below_it + rows_in, place])
                )
                outs.append(
                    copies.start(
                        r["ut_v"].at[pl.ds(b, rows_out), :],
                        target.at[below_it + rows_in : below_it + rows_in + rows_out, place],
                    )
                )

        def project():
            ready(wait_out)
            for k in range(width // TILE):
                t = cols(k)
                value = x[:, t] + mm(r["u_v"][...], wout[:, t])
                r["out_v"][:, t] = (value * mask).astype(BF16)
            save("out_o", r["out_v"])

        def backward():
            copy_g.wait()
            ready(loads)
            ready(wait_out)
            g = r["g_v"][...].astype(F32) * mask
            a_s, dact, dconv, dzx = r["a_v"], r["dact_v"], r["dconv_v"], r["dzx_v"]
            small = r["small_v"]
            if mode != "scan":
                gated_backward(g, a_s, dzx, small)
            if mode != "gated":
                scan_backward(g, a_s, dact, dconv, dzx, small)

        def gated_backward(g, a_s, dzx, small):
            r["dout_v"][...] = g.astype(BF16)
            target = r["all_o"] if "all_o" in r else r["head_o"]
            outs.append(copies.start(r["dout_v"], target.at[:, 0:width]))
            small[...] = jnp.zeros(small.shape, F32)
            total = jnp.zeros((seq, TILE), F32)
            mixed = jnp.zeros((seq, TILE), F32)
            for k in range(inner_tiles):
                t = cols(k)
                du = mm(r["dout_v"][...], wout[t, :], (1, 1))
                a_s[:, t] = du
                z = gate[:, t]
                gated = y_s[:, t] * (z * sigmoid(z))
                total = total + gated * gated
                mixed = mixed + du * pv[5:6, t] * gated
            back = lax.rsqrt(jnp.sum(total, axis=-1, keepdims=True) / INNER + EPS)
            pull = jnp.sum(mixed, axis=-1, keepdims=True) / INNER * back * back
            for k in range(inner_tiles):
                t = cols(k)
                z, y, du = gate[:, t], y_s[:, t], a_s[:, t]
                sig = sigmoid(z)
                act = z * sig
                gated = y * act
                small[5:6, t] = jnp.sum(du * gated * back, axis=0, keepdims=True)
                dgated = back * (du * pv[5:6, t] - gated * pull)
                a_s[:, t] = dgated * act
                dzx[:, t] = (dgated * y * (sig * (1.0 + z * (1.0 - sig)))).astype(BF16)
            target = r["all_o"] if "all_o" in r else r["head_o"]
            outs.append(copies.start(dzx.at[:, 0:INNER], target.at[:, width : width + INNER]))
            if mode == "gated":
                save("dy_o", a_s)
                save("small_o", small)

        def scan_backward(g, a_s, dact, dconv, dzx, small):
            dconv[seq : seq + PAD, :] = jnp.zeros((PAD, XBC), F32)
            v, dt, minus_a, rate, cum = steps(raw_s[...])
            cum_t, dt_t = cum.T, dt.T
            bmat = xs_s[:, INNER : INNER + STATE]
            cmat = xs_s[:, INNER + STATE : XBC]
            inner = mm(cmat, bmat, (1, 1))
            dinner = jnp.zeros((seq, seq), F32)
            dcum = jnp.zeros((seq, LANES), F32)
            dlast = jnp.zeros((seq, LANES), F32)
            dskip = jnp.zeros((PAD, LANES), F32)
            head_row = lax.broadcasted_iota(jnp.int32, (2 * LANES, LANES), 0)
            head_col = lax.broadcasted_iota(jnp.int32, (2 * LANES, LANES), 1)
            for p in range(pairs):
                t = cols(p, LANES)
                both, decays = [], []
                for head in (2 * p, 2 * p + 1):
                    diff = cum[:, head : head + 1] - cum_t[head : head + 1, :]
                    decay = jnp.exp(jnp.where(below, diff, -1e30))
                    both.append((inner * decay * dt_t[head : head + 1, :]).astype(BF16))
                    decays.append(decay * dt_t[head : head + 1, :])
                scores = jnp.concatenate(both, axis=1)
                xp = xs_s[:, t]
                none = jnp.zeros_like(xp)
                wide = jnp.concatenate(
                    [jnp.where(first_head, xp, none), jnp.where(first_head, none, xp)], axis=0
                )
                dy = a_s[:, t]
                dy_low = dy.astype(BF16)
                dscores = mm(dy_low, wide, (1, 1))
                dinner = dinner + dscores[:, 0:seq] * decays[0] + dscores[:, seq:] * decays[1]
                spread = mm(scores, dy_low, (0, 0))
                dxs = jnp.where(first_head, spread[0:seq], spread[seq:])
                xf = xp.astype(F32)
                skip = pv[8:9, t]
                dact[:, t] = dy * skip + dxs
                own = jnp.where(head_col == 2 * p + (head_row % LANES) // HEAD_DIM, 1.0, 0.0).astype(BF16)
                left = xf * dxs
                dlast = dlast + mm(jnp.concatenate(split_two(left), axis=1), own)
                gap = dy_low.astype(F32) * (y_s[:, t] - skip * xf) - left
                dcum = dcum + mm(jnp.concatenate(split_two(gap), axis=1), own)
                by_lane = jnp.sum(dy * xf, axis=0, keepdims=True)
                by_lane = jnp.broadcast_to(by_lane, (PAD, LANES))
                dskip = dskip + mm(jnp.concatenate(split_two(by_lane), axis=1), own)
            above = jnp.where(
                lax.broadcasted_iota(jnp.int32, (seq, seq), 0)
                <= lax.broadcasted_iota(jnp.int32, (seq, seq), 1),
                1.0,
                0.0,
            )
            drate = mm(above, dcum, precision=lax.Precision.HIGHEST)
            sig = sigmoid(v)
            ratio = jnp.where(v < -15.0, 1.0, sig / jnp.maximum(dt, 1e-30))
            draw = drate * minus_a * sig + dlast * ratio
            draw_low = draw.astype(BF16)
            dzx[:, INNER + XBC : INNER + XBC + LANES] = draw_low
            small[7:8, 0:LANES] = jnp.sum(draw, axis=0, keepdims=True)
            small[7:8, LANES : 2 * LANES] = jnp.sum(drate * rate, axis=0, keepdims=True)
            small[7:8, 2 * LANES : 3 * LANES] = dskip[0:1, :]
            dinner_low = dinner.astype(BF16)
            dact[:, INNER : INNER + STATE] = mm(dinner_low, cmat, (0, 0))
            dact[:, INNER + STATE : XBC] = mm(dinner_low, bmat)
            for k in range(conv_tiles):
                t = cols(k)
                conv = conv_tile(k)
                sig = sigmoid(conv)
                grad = dact[:, t] * (sig * (1.0 + conv * (1.0 - sig)))
                dconv[0:seq, t] = grad
                small[4:5, t] = jnp.sum(grad, axis=0, keepdims=True)
                dxbc = jnp.zeros((seq, TILE), F32)
                for tap in range(CONV):
                    start = PAD - (CONV - 1) + tap
                    small[tap : tap + 1, t] = jnp.sum(
                        grad * xbc[start : start + seq, t], axis=0, keepdims=True
                    )
                    ahead = CONV - 1 - tap
                    dxbc = dxbc + dconv[ahead : ahead + seq, t] * pv[tap : tap + 1, t]
                dzx[:, INNER + k * TILE : INNER + (k + 1) * TILE] = dxbc.astype(BF16)
            if "all_o" in r:
                target = r["all_o"].at[:, width + INNER : width + INNER + XBC + LANES]
                outs.append(copies.start(dzx.at[:, INNER : INNER + XBC + LANES], target))
            else:
                outs.append(copies.start(dzx.at[:, INNER : INNER + XBC + LANES], r["dside_o"]))
            dh = r["dh_v"]
            for waits in wait_in:
                ready(waits)
            for k in range(width // TILE):
                t = cols(k)
                dh[:, t] = mm(dzx[:, 0 : INNER + XBC], win[t, :], (1, 1)) + mm(draw_low, wdt[t, :], (1, 1))
            product = dh[...] * gain
            pulled = jnp.mean(product * x, axis=-1, keepdims=True) * scale * scale
            dx = g + scale * (product - x * pulled)
            small[6:7, 0:width] = jnp.sum(dh[...] * x * scale, axis=0, keepdims=True)
            dh[...] = dx
            r["dxb_v"][...] = dx.astype(BF16)
            if "dxb_o" in r:
                save("dxb_o", r["dxb_v"])
            save("dx_o", dh)
            save("small_o", small)

        if mode in ("start", "fwd", "both"):
            forward()
        if mode == "out":
            ready(loads)
        if mode in ("out", "fwd", "both"):
            project()
        if mode in ("both", "bwd", "gated", "scan"):
            backward()
        finish_outs()

    pl.when(lax.axis_index("section") == cfg["section"])(body)


RESIDUALS = ("gate", "xbc", "y", "raw", "xs")
COST = dict(start=8000, out=2000, fwd=9000, both=18000, bwd=13000, gated=5000, scan=10000)
RESIDUALS_USED = dict(
    bwd=RESIDUALS, gated=("gate", "y"), scan=("raw", "xs", "dy", "y", "xbc", "small", "head"), out=("u",)
)


def layer_call(
    name,
    section,
    slot,
    block,
    mode,
    args,
    weights,
    residual=None,
    kept=None,
    save=False,
    one_array=False,
    ahead=(),
):
    win, wout, wdt, pv = weights
    kept = kept or {}
    n = args["pieces"]
    seq, width = args["tok"].shape[1], args["tok"].shape[2]
    rows = width // n + INNER // n
    proj = INNER + XBC
    shapes = dict(
        gate=((seq, INNER), F32),
        xbc=((seq, XBC), F32),
        y=((seq, INNER), F32),
        raw=((seq, LANES), F32),
        xs=((seq, XBC), BF16),
        out=((seq, width), BF16),
        u=((seq, INNER), BF16),
        dy=((seq, INNER), F32),
        all=((seq, width + proj + LANES), BF16),
        head=((seq, width + INNER), BF16),
        dside=((seq, XBC + LANES), BF16),
        dx=((seq, width), F32),
        dxb=((seq, width), BF16),
        small=((8, XBC), F32),
    )
    for k in range(min(n, 2)):
        shapes[f"hu{k}"] = ((rows * (2 if n > 1 else 1), 2 * seq), BF16)
    inputs = [("lengths", args["lengths"], pl.BlockSpec(memory_space=pltpu.SMEM))]
    inputs.append(("tok", args["tok"], FAR) if section == 0 else ("arr", args["arr"], ANY))
    if mode in ("both", "bwd", "gated", "scan"):
        inputs.append(("cot", args["cot"], FAR) if section == 1 else ("arrg", args["arrg"], ANY))
    if mode not in ("out", "gated"):
        inputs += [(f"win{k}", w, FAR) for k, w in enumerate(win)]
    if mode != "out":
        inputs += [("wdt", wdt, FAR), ("pv", pv, FAR)]
    if mode not in ("start", "scan"):
        inputs += [(f"wout{k}", w, FAR) for k, w in enumerate(wout)]
    inputs += [(f"{k}_i", residual[k], FAR) for k in RESIDUALS_USED.get(mode, ())]
    inputs += [(f"ahead{k}", value, FAR) for k, value in enumerate(ahead)]
    outputs = []
    if mode in ("start", "fwd", "both"):
        outputs += [f"hu{k}" for k in range(min(n, 2))]
        if save:
            outputs += list(RESIDUALS)
    if mode == "start":
        outputs.append("u")
    if mode in ("out", "fwd", "both"):
        outputs.append("out")
    if mode in ("both", "bwd"):
        outputs += ["all"] if one_array else ["head", "dside"]
        outputs += ["dx", "small"]
        if section == 1:
            outputs.append("dxb")
    if mode == "gated":
        outputs += ["head", "dy", "small"]
    if mode == "scan":
        outputs += ["dside", "dx", "small"]
    aliases = {}
    for place, key in enumerate(outputs):
        if key in kept:
            aliases[len(inputs)] = place
            inputs.append((f"{key}_k", kept[key], FAR))
    scratch = dict(
        x_v=((seq, width), BF16),
        g_v=((seq, width), BF16),
        dout_v=((seq, width), BF16),
        out_v=((seq, width), BF16),
        dxb_v=((seq, width), BF16),
        win_v=((width, proj), BF16),
        wout_v=((INNER, width), BF16),
        wdt_v=((width, LANES), BF16),
        pv_v=(pv.shape, F32),
        gate_v=((seq, INNER), F32),
        xbc_v=((seq + PAD, XBC), F32),
        y_v=((seq, INNER), F32),
        raw_v=((seq, LANES), F32),
        xs_v=((seq, XBC), BF16),
        ht_v=((width, seq), BF16),
        u_v=((seq, INNER), BF16),
        ut_v=((INNER, seq), BF16),
        a_v=((seq, INNER), F32),
        dact_v=((seq, XBC), F32),
        dconv_v=((seq + PAD, XBC), F32),
        dzx_v=((seq, proj + LANES), BF16),
        dh_v=((seq, width), F32),
        small_v=((8, XBC), F32),
    )
    names = [k for k, _, _ in inputs] + [f"{k}_o" for k in outputs] + list(scratch) + ["sems"]
    cfg = dict(
        names=names, pieces=n, section=section, slot=slot, block=block, mode=mode, seq=seq, width=width
    )
    results = pl.pallas_call(
        functools.partial(layer_kernel, cfg),
        out_shape=[jax.ShapeDtypeStruct(*shapes[k]) for k in outputs],
        in_specs=[spec for _, _, spec in inputs],
        out_specs=[FAR for _ in outputs],
        scratch_shapes=[pltpu.VMEM(*v) for v in scratch.values()]
        + [pltpu.SemaphoreType.DMA((96,))],
        input_output_aliases=aliases,
        cost_estimate=pl.CostEstimate(flops=COST[mode] * 10**6, bytes_accessed=10**6, transcendentals=0),
        compiler_params=pltpu.CompilerParams(vmem_limit_bytes=VMEM_LIMIT),
        name=name,
    )(*[value for _, value, _ in inputs])
    return dict(zip(outputs, results))


def product_kernel(rows, places, parts, count, extra, *refs):
    lefts, first, second = refs[:count], refs[count : 2 * count], refs[2 * count : 3 * count]
    smalls = refs[3 * count : 3 * count + extra]
    outs, (left_v, right_v, small_v, sems) = refs[-4 - len(parts) : -4], refs[-4:]
    seq = first[0].shape[0]
    copies = Copies(sems)
    waits = []
    for k in range(count):
        start = 2 * k * seq
        waits.append(copies.start(lefts[k].at[rows, :], left_v.at[:, start : start + 2 * seq]))
        for slot, side in enumerate((first[k], second[k])):
            at = start + slot * seq
            waits.append(copies.start(side.at[:, places[slot]], right_v.at[at : at + seq, :]))
    for k in range(extra):
        waits.append(copies.start(smalls[k], small_v.at[k]))
    for copy in waits:
        copy.wait()
    if extra:
        total = small_v[0]
        for k in range(1, extra):
            total = total + small_v[k]
        half = total.shape[1] // 2
        total = jnp.concatenate([total[:, :half], total[:, half:]], axis=0)
        for out in outs[0:2]:
            out[out.shape[0] - 16 :, 0:half] = total.astype(out.dtype)
            out[out.shape[0] - 16 :, half:] = jnp.zeros((16, out.shape[1] - half), out.dtype)
    for out, (height, above, at, size) in zip(outs, parts):
        for k in range(0, size, TILE):
            end = min(k + TILE, size)
            value = mm(left_v[above : above + height, :], right_v[:, at + k : at + end])
            out[0:height, k:end] = value.astype(out.dtype)


def weight_product(name, lefts, rows, first, second, places, parts, ahead=(), smalls=()):
    count = len(lefts)
    depth = 2 * count * first[0].shape[0]
    tall, wide = rows.stop - rows.start, places[0].stop - places[0].start
    shapes = [(part[0], part[3]) for part in parts]
    if smalls:
        shapes[:2] = [(height + 16, size) for height, size in shapes[:2]]
    return pl.pallas_call(
        functools.partial(product_kernel, rows, places, parts, count, len(smalls)),
        out_shape=[jax.ShapeDtypeStruct(shape, BF16) for shape in shapes],
        in_specs=[FAR] * (3 * count + len(smalls) + len(ahead)),
        out_specs=[pl.BlockSpec(memory_space=pltpu.VMEM) for _ in shapes],
        scratch_shapes=[
            pltpu.VMEM((tall, depth), BF16),
            pltpu.VMEM((depth, wide), BF16),
            pltpu.VMEM((2, 8, XBC), F32),
            pltpu.SemaphoreType.DMA((3 * count + 2,)),
        ],
        cost_estimate=pl.CostEstimate(flops=10**6, bytes_accessed=10**6, transcendentals=0),
        compiler_params=pltpu.CompilerParams(vmem_limit_bytes=VMEM_LIMIT),
        name=name,
    )(*lefts, *first, *second, *smalls, *ahead)


def across(block, axis, way):
    size = lax.axis_size(axis)
    route = [(i, i + way) for i in range(size) if 0 <= i + way < size]
    return lax.ppermute(block, axis, route)


def swap(block, axis, bits):
    size = lax.axis_size(axis)
    return lax.ppermute(block, axis, [(i, i ^ bits) for i in range(size)])


def after(value, *others):
    return lax.optimization_barrier((value,) + others)[0]


def spread(own):
    far = swap(own, "fsdp", 2)
    return [own, swap(own, "fsdp", 1), far, swap(far, "fsdp", 1)]


def beside(own):
    return [own, swap(own, "fsdp", 1)]


def quarter(value, parts, number):
    rows = value.shape[0] // parts
    return lax.dynamic_slice_in_dim(value, number * rows, rows, axis=0)


def in_order(pieces, me):
    odd, high = (me & 1) == 1, (me & 2) == 2
    a = jnp.where(odd, pieces[1], pieces[0])
    b = jnp.where(odd, pieces[0], pieces[1])
    c = jnp.where(odd, pieces[3], pieces[2])
    d = jnp.where(odd, pieces[2], pieces[3])
    low = [jnp.where(high, c, a), jnp.where(high, d, b)]
    return jnp.stack(low + [jnp.where(high, a, c), jnp.where(high, b, d)])


def group_sums(own_parts, far_parts, place):
    middle = (place == 1) | (place == 2)
    count = len(own_parts)
    arrived, halves, totals, outwards = [], [], [], []

    def done(values, k):
        return [values[k]] if 0 <= k < len(values) else []

    for step in range(count + 2):
        if step < count:
            far = after(far_parts[step], *done(arrived, step - 2), *done(halves, step - 3))
            arrived.append(swap(far, "fsdp", 2))
        k = step - 1
        if 0 <= k < count:
            own = (own_parts[k].astype(F32) + arrived[k].astype(F32)).astype(BF16)
            own = after(own, *done(halves, k - 2))
            inward = lax.ppermute(own, "dp", [(0, 1), (3, 2)])
            inward = after(inward, *done(arrived, k + 1), *done(totals, k - 2))
            halves.append((own.astype(F32) + inward.astype(F32)).astype(BF16))
        k = step - 2
        if 0 <= k < count:
            other = lax.ppermute(halves[k], "dp", [(1, 2), (2, 1)])
            other = after(other, *done(halves, k + 1), *done(outwards, k - 2))
            totals.append((halves[k].astype(F32) + other.astype(F32)).astype(BF16))
            outwards.append(lax.ppermute(totals[k], "dp", [(1, 0), (2, 3)]))
    return [jnp.where(middle, t, o).astype(F32) for t, o in zip(totals, outwards)]


def on_device(
    tokens,
    cotangent,
    lengths,
    norm_gain,
    in_weight,
    dt_weight,
    conv_weight,
    conv_bias,
    dt_bias,
    a_log,
    skip,
    gated_gain,
    out_weight,
):
    n = lax.axis_size("fsdp")
    square = n == 4 and lax.axis_size("dp") == 4
    section = lax.axis_index("section")
    me = lax.axis_index("fsdp")
    seq, width = tokens.shape[1], tokens.shape[2]
    proj = INNER + XBC
    if square:
        in_pair = lax.axis_index("dp") & 1
        fetched = [quarter(in_weight[0], 4, 2 * in_pair + k) for k in range(2)]
        over = [swap(fetched[0], "fsdp", 2)]
        norm_gain = after(norm_gain, over[0], fetched[1])
        over.append(swap(fetched[1], "fsdp", 2))
    smalls = (norm_gain, conv_weight, conv_bias, dt_bias, a_log, skip, gated_gain, dt_weight)
    packed = jnp.concatenate([s[0].reshape(-1) for s in smalls])
    if square:
        win = [in_weight[0], swap(in_weight[0], "fsdp", 1)]
        past = [swap(part, "dp", 1) for part in over]
        win += [part for pair in zip(over, past) for part in pair]
        win += [swap(part, "fsdp", 1) for part in win[2:]]
        lengths, packed = lax.optimization_barrier((lengths.reshape(-1), packed))
        over_out = swap(quarter(after(out_weight[0], past[0], over[1]), 2, in_pair), "fsdp", 2)
        far_out = [over_out, swap(over_out, "dp", 1)]
        packed = in_order(spread(after(packed, past[0])), me)
    else:
        win = [lax.all_gather(in_weight[0], "fsdp", axis=0, tiled=True)]
        wout = [lax.all_gather(out_weight[0], "fsdp", axis=0, tiled=True)]
        packed = lax.all_gather(packed, "fsdp", axis=0)
        lengths = lengths.reshape(-1)
    parts, place = [], 0
    for s in smalls:
        size = s.size
        parts.append(packed[:, place : place + size].reshape((n,) + s.shape[1:]))
        place += size

    def row(v, size=XBC):
        v = v.reshape(1, -1).astype(F32)
        return jnp.pad(v, ((0, 0), (0, size - v.shape[1])))

    conv_w = parts[1].transpose(1, 0, 2).reshape(CONV, XBC).astype(F32)
    sevens = jnp.concatenate([row(parts[3], LANES), row(parts[4], LANES), row(parts[5], LANES)], axis=1)
    pv = jnp.concatenate(
        [
            conv_w,
            row(parts[2]),
            row(parts[6]),
            row(parts[0]),
            row(sevens),
            row(jnp.repeat(parts[5].reshape(-1), HEAD_DIM)),
            jnp.zeros((7, XBC), F32),
        ]
    )
    wdt = jnp.pad(parts[7].reshape(width, HEADS), ((0, 0), (0, LANES - HEADS)))

    def keep(done, *keys):
        return {k: done[k] for k in done if k.startswith(keys)}

    at_zero = section == 0
    pieces = n if square else 1
    args = dict(tok=tokens, cot=cotangent, lengths=lengths, pieces=pieces)
    fwd_p = layer_call("start_p", 0, 0, 0, "start", args, (win, [], wdt, pv), save=True)
    if square:
        wout = [out_weight[0], swap(out_weight[0], "fsdp", 1), *far_out]
        wout += [swap(after(part, fwd_p["u"]), "fsdp", 1) for part in far_out]
    weights = (win, wout, wdt, pv)
    fwd_p.update(layer_call("out_p", 0, 0, 0, "out", args, weights, fwd_p))
    args["arr"] = across(fwd_p["out"], "section", 1)
    fwd_q = layer_call("fwd_q", 0, 1, 1, "fwd", args, weights, kept=keep(fwd_p, "hu"), save=True)
    arr_p = across(fwd_q["out"], "section", 1)
    both_q = layer_call("both_q", 1, 1, 0, "both", args, weights, kept=keep(fwd_q, "hu"))
    args["arrg"] = across(both_q["dxb"], "section", -1)
    args["arr"] = arr_p
    both_p = layer_call("both_p", 1, 0, 1, "both", args, weights, kept=keep(both_q, "hu"), one_array=True)
    arrg_q = across(both_p["dxb"], "section", -1)
    bwd_p = layer_call(
        "bwd_p", 0, 0, 0, "bwd", args, weights, fwd_p, keep(both_p, "all", "dx", "small"),
        one_array=True,
    )
    args["arrg"] = arrg_q
    gated_q = layer_call(
        "gated_q", 0, 1, 1, "gated", args, weights, fwd_q, keep(both_q, "head"),
        ahead=[bwd_p["dx"]],
    )
    rows_in, rows_out = width // pieces, INNER // pieces
    height = rows_in + rows_out
    hu, all_p, head_q = [both_p["hu0"]], [bwd_p["all"]], [gated_q["head"]]
    bases = (0,)
    if square:
        hu, all_p, head_q = hu + [swap(both_p["hu1"], "fsdp", 1)], beside(all_p[0]), beside(head_q[0])
        bases = (0, height)

    def parts_of(*parts):
        return tuple((size, base + row, at, wide) for size, row, at, wide in parts for base in bases)

    places = (slice(0, width + INNER),) * 2
    head_parts = (
        (rows_out // 2, rows_in, 0, width),
        (rows_out // 2, rows_in + rows_out // 2, 0, width),
        (rows_in, 0, width, INNER // 2),
        (rows_in, 0, width + INNER // 2, INNER // 2),
    )
    if not square:
        head_parts = ((rows_out, rows_in, 0, width), *head_parts[2:])
    parts = parts_of(*head_parts)
    grads = weight_product("grad_head", hu, slice(0, height * len(bases)), all_p, head_q, places, parts)
    scan_q = layer_call(
        "scan_q", 0, 1, 1, "scan", args, weights, {**fwd_q, **gated_q},
        keep(both_q, "dside", "dx", "small"), ahead=grads[:1],
    )
    small = bwd_p["small"] + scan_q["small"]
    side_q, smalls, ahead = [scan_q["dside"]], [], ()
    if square:
        side_q, smalls = beside(side_q[0]), beside(small)
    places = (slice(width + INNER, width + proj + LANES), slice(0, XBC + LANES))
    parts = parts_of((rows_in, 0, 0, CUT), (rows_in, 0, CUT, XBC + LANES - CUT))
    grads += weight_product(
        "grad_side", hu, slice(0, height * len(bases)), all_p, side_q, places, parts, (), smalls
    )

    def by_block(p, q):
        return jnp.stack([jnp.where(at_zero, p, q), jnp.where(at_zero, q, p)])

    outputs = by_block(
        jnp.where(at_zero, fwd_p["out"], both_p["out"]), jnp.where(at_zero, fwd_q["out"], both_q["out"])
    )
    input_grads = by_block(bwd_p["dx"], scan_q["dx"])
    if square:
        line = lax.axis_index("dp")
        grads = group_sums(grads[0::2], grads[1::2], line)
        small = grads[-2][rows_in:, : XBC // 2]
        small = jnp.concatenate([small[:8], small[8:]], axis=1)
    else:
        grads = [lax.psum_scatter(g, "fsdp", scatter_dimension=0, tiled=True) for g in grads]
        grads = [g.astype(F32) for g in lax.psum(grads, "dp")]
        small = lax.psum(small, ("dp", "fsdp"))
    *grad_out, gate_low, gate_high, grad_near, grad_rest = grads
    rows_own = width // n

    def own(v):
        size = v.shape[-1] // n
        return lax.dynamic_slice_in_dim(v, me * size, size, axis=v.ndim - 1)

    return (
        outputs[None],
        input_grads[None],
        own(small[6:7, :width]),
        jnp.concatenate([gate_low, gate_high, grad_near[:rows_own], grad_rest[:, : XBC - CUT]], axis=1)[None],
        grad_rest[None, :, XBC - CUT : XBC - CUT + HEADS],
        own(small[None, 0:CONV]),
        own(small[4:5]),
        own(small[7:8, 0:HEADS]),
        own(small[7:8, LANES : LANES + HEADS]),
        own(small[7:8, 2 * LANES : 2 * LANES + HEADS]),
        own(small[5:6, :INNER]),
        jnp.concatenate(grad_out)[None],
    )


def solution(mesh):
    in_specs = (
        P(None, ("dp", "fsdp"), None),
        P(None, ("dp", "fsdp"), None),
        P(None, ("dp", "fsdp")),
        P("section", "fsdp"),
        P("section", "fsdp", None),
        P("section", "fsdp", None),
        P("section", None, "fsdp"),
        P("section", "fsdp"),
        P("section", "fsdp"),
        P("section", "fsdp"),
        P("section", "fsdp"),
        P("section", "fsdp"),
        P("section", "fsdp", None),
    )
    out_specs = (
        P("section", None, ("dp", "fsdp"), None),
        P("section", None, ("dp", "fsdp"), None),
        P("section", "fsdp"),
        P("section", "fsdp", None),
        P("section", "fsdp", None),
        P("section", None, "fsdp"),
        P("section", "fsdp"),
        P("section", "fsdp"),
        P("section", "fsdp"),
        P("section", "fsdp"),
        P("section", "fsdp"),
        P("section", "fsdp", None),
    )
    return jax.shard_map(
        on_device, mesh=mesh, in_specs=in_specs, out_specs=out_specs, check_vma=False
    )
```

```python
import functools

import jax
import jax.numpy as jnp
from jax import lax
from jax.experimental import pallas as pl
from jax.experimental.pallas import tpu as pltpu
from jax.sharding import PartitionSpec as P

INNER = 1536
HEADS = 24
STATE = 128
HEAD_DIM = 64
CONV = 4
XBC = 1792
LANES = 128
TILE = 256
PAD = 8
CUT = 1024
WIN_CUTS = (slice(0, 512), slice(512, 1536), slice(1536, 3328))

EPS = 1e-05
F32 = jnp.float32
BF16 = jnp.bfloat16
ANY = pl.BlockSpec(memory_space=pl.ANY)
FAR = pl.BlockSpec(memory_space=pltpu.HBM)
VMEM_LIMIT = 60 * 1024 * 1024


def mm(a, b, contract=(1, 0), precision=None):
    dims = (((contract[0],), (contract[1],)), ((), ()))
    return lax.dot_general(a, b, dims, precision=precision, preferred_element_type=F32)


def sigmoid(v):
    return 1.0 / (1.0 + jnp.exp(-v))


def split_two(v):
    high = v.astype(BF16)
    return high, (v - high.astype(F32)).astype(BF16)


class Copies:
    def __init__(self, sems):
        self.sems = sems
        self.used = 0

    def make(self, source, target):
        copy = pltpu.make_async_copy(source, target, self.sems.at[self.used])
        self.used += 1
        return copy

    def start(self, source, target):
        copy = self.make(source, target)
        copy.start()
        return copy


def layer_kernel(cfg, *refs):
    r = dict(zip(cfg["names"], refs))
    n = cfg["pieces"]
    mode, block = cfg["mode"], cfg["block"]
    seq, width = cfg["seq"], cfg["width"]
    rows_in, rows_out = width // n, INNER // n
    order = [0]
    if n > 1:
        me = lax.axis_index("fsdp")
        order = [me ^ k for k in range(n)]
        pair = lax.axis_index("dp") & 1
    length = r["lengths"][block]
    in_places = [(order[k] * rows_in, rows_in) for k in range(min(n, 2))]
    out_places = [(order[k] * rows_out, rows_out) for k in range(min(n, 2))]
    if n > 1:
        for k in (2, 3):
            for part in range(4):
                number = 2 * (pair ^ (part & 1)) + part // 2
                in_places.append((order[k] * rows_in + number * (rows_in // 4), rows_in // 4))
            for part in range(2):
                out_places.append((order[k] * rows_out + (pair ^ part) * (rows_out // 2), rows_out // 2))
    win, wout, wdt, pv = r["win_v"], r["wout_v"], r["wdt_v"], r["pv_v"]
    gate, xbc, y_s, raw_s, xs_s = r["gate_v"], r["xbc_v"], r["y_v"], r["raw_v"], r["xs_v"]
    inner_tiles = INNER // TILE
    conv_tiles = XBC // TILE
    pairs = INNER // LANES
    copies = Copies(r["sems"])

    def cols(k, size=TILE):
        return slice(k * size, (k + 1) * size)

    def body():
        copy_x = copies.start(r["tok"].at[block] if cfg["section"] == 0 else r["arr"], r["x_v"])
        copy_g, loads, wait_in, wait_out, params = None, [], [], [], []

        def load_in():
            for t in WIN_CUTS:
                waits = []
                for k, (row, rows) in enumerate(in_places):
                    row = pl.multiple_of(row, 16)
                    waits.append(copies.start(r[f"win{k}"].at[:, t], win.at[pl.ds(row, rows), t]))
                wait_in.append(waits)

        def load_out():
            for k, (row, rows) in enumerate(out_places):
                row = pl.multiple_of(row, 16)
                wait_out.append(copies.start(r[f"wout{k}"], wout.at[pl.ds(row, rows), :]))

        if mode != "out":
            params = [copies.start(r["pv"], pv), copies.start(r["wdt"], wdt)]
        if mode in ("both", "bwd", "gated", "scan"):
            copy_g = copies.start(r["cot"].at[block] if cfg["section"] == 1 else r["arrg"], r["g_v"])
        if mode == "bwd":
            load_out()
            loads = [
                copies.start(r["gate_i"], gate),
                copies.start(r["y_i"], y_s),
                copies.start(r["raw_i"], raw_s),
                copies.start(r["xs_i"], xs_s),
                copies.start(r["xbc_i"], xbc.at[PAD : PAD + seq, :]),
            ]
            load_in()
        elif mode == "gated":
            load_out()
            loads = [copies.start(r["gate_i"], gate), copies.start(r["y_i"], y_s)]
        elif mode == "scan":
            loads = [
                copies.start(r["raw_i"], raw_s),
                copies.start(r["xs_i"], xs_s),
                copies.start(r["dy_i"], r["a_v"]),
                copies.start(r["y_i"], y_s),
                copies.start(r["xbc_i"], xbc.at[PAD : PAD + seq, :]),
                copies.start(r["small_i"], r["small_v"]),
                copies.start(r["head_i"].at[:, width : width + INNER], r["dzx_v"].at[:, 0:INNER]),
            ]
            load_in()
        elif mode == "out":
            loads = [copies.start(r["u_i"], r["u_v"])]
            load_out()
        else:
            load_in()
            if mode != "start":
                load_out()

        def ready(waits):
            for copy in waits:
                copy.wait()
            waits.clear()

        below = lax.broadcasted_iota(jnp.int32, (seq, seq), 0) >= lax.broadcasted_iota(
            jnp.int32, (seq, seq), 1
        )
        row_id = lax.broadcasted_iota(jnp.int32, (seq, 1), 0)
        mask = jnp.where(row_id < length, 1.0, 0.0)
        lane = lax.broadcasted_iota(jnp.int32, (seq, LANES), 1)
        first_head = lane < HEAD_DIM
        xbc[0:PAD, :] = jnp.zeros((PAD, XBC), F32)
        copy_x.wait()
        ready(params)
        x = r["x_v"][...].astype(F32)
        scale = lax.rsqrt(jnp.mean(x * x, axis=-1, keepdims=True) + EPS)
        gain = pv[6:7, 0:width]
        outs = []

        def save(name, source):
            if name in r:
                outs.append(copies.start(source, r[name]))

        def finish_outs():
            for copy in outs:
                copy.wait()
            outs.clear()

        def conv_tile(k):
            t = cols(k)
            conv = pv[4:5, t]
            for tap in range(CONV):
                start = PAD - (CONV - 1) + tap
                conv = conv + xbc[start : start + seq, t] * pv[tap : tap + 1, t]
            return conv

        def steps(value):
            v = value + pv[7:8, 0:LANES]
            small = jnp.exp(-jnp.abs(v))
            dt = jnp.maximum(v, 0.0) + jnp.log1p(small)
            minus_a = -jnp.exp(pv[7:8, LANES : 2 * LANES])
            rate = dt * minus_a
            ones = jnp.where(below, 1.0, 0.0)
            cum = mm(ones, rate, precision=lax.Precision.HIGHEST)
            return v, dt, minus_a, rate, cum

        def forward():
            h = (x * scale * gain).astype(BF16)
            for waits, cut in zip(wait_in, WIN_CUTS):
                ready(waits)
                for start in range(cut.start, cut.stop, TILE):
                    value = mm(h, win[:, start : start + TILE])
                    if start < INNER:
                        gate[:, start : start + TILE] = value
                    else:
                        xbc[PAD : PAD + seq, start - INNER : start - INNER + TILE] = value
            raw = mm(h, wdt[...])
            raw_s[...] = raw
            save("gate_o", gate)
            save("xbc_o", xbc.at[PAD : PAD + seq, :])
            save("raw_o", raw_s)
            h_t = h.T
            r["ht_v"][...] = h_t
            for k in range(conv_tiles):
                conv = conv_tile(k)
                xs_s[:, cols(k)] = (conv * sigmoid(conv)).astype(BF16)
            save("xs_o", xs_s)
            _, dt, _, _, cum = steps(raw)
            cum_t, dt_t = cum.T, dt.T
            bmat = xs_s[:, INNER : INNER + STATE]
            cmat = xs_s[:, INNER + STATE : XBC]
            inner = mm(cmat, bmat, (1, 1))
            total = jnp.zeros((seq, LANES), F32)
            gated_v = r["a_v"]
            for p in range(pairs):
                t = cols(p, LANES)
                both = []
                for head in (2 * p, 2 * p + 1):
                    diff = cum[:, head : head + 1] - cum_t[head : head + 1, :]
                    decay = jnp.exp(jnp.where(below, diff, -1e30))
                    both.append((inner * decay * dt_t[head : head + 1, :]).astype(BF16))
                xp = xs_s[:, t]
                none = jnp.zeros_like(xp)
                wide = jnp.concatenate(
                    [jnp.where(first_head, xp, none), jnp.where(first_head, none, xp)], axis=0
                )
                y = mm(jnp.concatenate(both, axis=1), wide) + xp.astype(F32) * pv[8:9, t]
                y_s[:, t] = y
                z = gate[:, t]
                gated = y * (z * sigmoid(z))
                gated_v[:, t] = gated
                total = total + gated * gated
            save("y_o", y_s)
            back = lax.rsqrt(jnp.sum(total, axis=-1, keepdims=True) / INNER + EPS)
            for p in range(inner_tiles):
                t = cols(p)
                u = (gated_v[:, t] * back * pv[5:6, t]).astype(BF16)
                r["u_v"][:, t] = u
                r["ut_v"][t, :] = u.T
            save("u_o", r["u_v"])
            for k in range(n):
                a = pl.multiple_of(order[k] * rows_in, 16)
                b = pl.multiple_of(order[k] * rows_out, 16)
                target, below_it = r[f"hu{k % 2}_o"], (rows_in + rows_out) * (k // 2)
                place = slice(cfg["slot"] * seq, (cfg["slot"] + 1) * seq)
                outs.append(
                    copies.start(r["ht_v"].at[pl.ds(a, rows_in), :], target.at[below_it : below_it + rows_in, place])
                )
                outs.append(
                    copies.start(
                        r["ut_v"].at[pl.ds(b, rows_out), :],
                        target.at[below_it + rows_in : below_it + rows_in + rows_out, place],
                    )
                )

        def project():
            ready(wait_out)
            for k in range(width // TILE):
                t = cols(k)
                value = x[:, t] + mm(r["u_v"][...], wout[:, t])
                r["out_v"][:, t] = (value * mask).astype(BF16)
            save("out_o", r["out_v"])

        def backward():
            copy_g.wait()
            ready(loads)
            ready(wait_out)
            g = r["g_v"][...].astype(F32) * mask
            a_s, dact, dconv, dzx = r["a_v"], r["dact_v"], r["dconv_v"], r["dzx_v"]
            small = r["small_v"]
            if mode != "scan":
                gated_backward(g, a_s, dzx, small)
            if mode != "gated":
                scan_backward(g, a_s, dact, dconv, dzx, small)

        def gated_backward(g, a_s, dzx, small):
            r["dout_v"][...] = g.astype(BF16)
            target = r["all_o"] if "all_o" in r else r["head_o"]
            outs.append(copies.start(r["dout_v"], target.at[:, 0:width]))
            small[...] = jnp.zeros(small.shape, F32)
            total = jnp.zeros((seq, TILE), F32)
            mixed = jnp.zeros((seq, TILE), F32)
            for k in range(inner_tiles):
                t = cols(k)
                du = mm(r["dout_v"][...], wout[t, :], (1, 1))
                a_s[:, t] = du
                z = gate[:, t]
                gated = y_s[:, t] * (z * sigmoid(z))
                total = total + gated * gated
                mixed = mixed + du * pv[5:6, t] * gated
            back = lax.rsqrt(jnp.sum(total, axis=-1, keepdims=True) / INNER + EPS)
            pull = jnp.sum(mixed, axis=-1, keepdims=True) / INNER * back * back
            for k in range(inner_tiles):
                t = cols(k)
                z, y, du = gate[:, t], y_s[:, t], a_s[:, t]
                sig = sigmoid(z)
                act = z * sig
                gated = y * act
                small[5:6, t] = jnp.sum(du * gated * back, axis=0, keepdims=True)
                dgated = back * (du * pv[5:6, t] - gated * pull)
                a_s[:, t] = dgated * act
                dzx[:, t] = (dgated * y * (sig * (1.0 + z * (1.0 - sig)))).astype(BF16)
            target = r["all_o"] if "all_o" in r else r["head_o"]
            outs.append(copies.start(dzx.at[:, 0:INNER], target.at[:, width : width + INNER]))
            if mode == "gated":
                save("dy_o", a_s)
                save("small_o", small)

        def scan_backward(g, a_s, dact, dconv, dzx, small):
            dconv[seq : seq + PAD, :] = jnp.zeros((PAD, XBC), F32)
            v, dt, minus_a, rate, cum = steps(raw_s[...])
            cum_t, dt_t = cum.T, dt.T
            bmat = xs_s[:, INNER : INNER + STATE]
            cmat = xs_s[:, INNER + STATE : XBC]
            inner = mm(cmat, bmat, (1, 1))
            dinner = jnp.zeros((seq, seq), F32)
            dcum = jnp.zeros((seq, LANES), F32)
            dlast = jnp.zeros((seq, LANES), F32)
            dskip = jnp.zeros((PAD, LANES), F32)
            head_row = lax.broadcasted_iota(jnp.int32, (2 * LANES, LANES), 0)
            head_col = lax.broadcasted_iota(jnp.int32, (2 * LANES, LANES), 1)
            for p in range(pairs):
                t = cols(p, LANES)
                both, decays = [], []
                for head in (2 * p, 2 * p + 1):
                    diff = cum[:, head : head + 1] - cum_t[head : head + 1, :]
                    decay = jnp.exp(jnp.where(below, diff, -1e30))
                    both.append((inner * decay * dt_t[head : head + 1, :]).astype(BF16))
                    decays.append(decay * dt_t[head : head + 1, :])
                scores = jnp.concatenate(both, axis=1)
                xp = xs_s[:, t]
                none = jnp.zeros_like(xp)
                wide = jnp.concatenate(
                    [jnp.where(first_head, xp, none), jnp.where(first_head, none, xp)], axis=0
                )
                dy = a_s[:, t]
                dy_low = dy.astype(BF16)
                dscores = mm(dy_low, wide, (1, 1))
                dinner = dinner + dscores[:, 0:seq] * decays[0] + dscores[:, seq:] * decays[1]
                spread = mm(scores, dy_low, (0, 0))
                dxs = jnp.where(first_head, spread[0:seq], spread[seq:])
                xf = xp.astype(F32)
                skip = pv[8:9, t]
                dact[:, t] = dy * skip + dxs
                own = jnp.where(head_col == 2 * p + (head_row % LANES) // HEAD_DIM, 1.0, 0.0).astype(BF16)
                left = xf * dxs
                dlast = dlast + mm(jnp.concatenate(split_two(left), axis=1), own)
                gap = dy_low.astype(F32) * (y_s[:, t] - skip * xf) - left
                dcum = dcum + mm(jnp.concatenate(split_two(gap), axis=1), own)
                by_lane = jnp.sum(dy * xf, axis=0, keepdims=True)
                by_lane = jnp.broadcast_to(by_lane, (PAD, LANES))
                dskip = dskip + mm(jnp.concatenate(split_two(by_lane), axis=1), own)
            above = jnp.where(
                lax.broadcasted_iota(jnp.int32, (seq, seq), 0)
                <= lax.broadcasted_iota(jnp.int32, (seq, seq), 1),
                1.0,
                0.0,
            )
            drate = mm(above, dcum, precision=lax.Precision.HIGHEST)
            sig = sigmoid(v)
            ratio = jnp.where(v < -15.0, 1.0, sig / jnp.maximum(dt, 1e-30))
            draw = drate * minus_a * sig + dlast * ratio
            draw_low = draw.astype(BF16)
            dzx[:, INNER + XBC : INNER + XBC + LANES] = draw_low
            small[7:8, 0:LANES] = jnp.sum(draw, axis=0, keepdims=True)
            small[7:8, LANES : 2 * LANES] = jnp.sum(drate * rate, axis=0, keepdims=True)
            small[7:8, 2 * LANES : 3 * LANES] = dskip[0:1, :]
            dinner_low = dinner.astype(BF16)
            dact[:, INNER : INNER + STATE] = mm(dinner_low, cmat, (0, 0))
            dact[:, INNER + STATE : XBC] = mm(dinner_low, bmat)
            for k in range(conv_tiles):
                t = cols(k)
                conv = conv_tile(k)
                sig = sigmoid(conv)
                grad = dact[:, t] * (sig * (1.0 + conv * (1.0 - sig)))
                dconv[0:seq, t] = grad
                small[4:5, t] = jnp.sum(grad, axis=0, keepdims=True)
                dxbc = jnp.zeros((seq, TILE), F32)
                for tap in range(CONV):
                    start = PAD - (CONV - 1) + tap
                    small[tap : tap + 1, t] = jnp.sum(
                        grad * xbc[start : start + seq, t], axis=0, keepdims=True
                    )
                    ahead = CONV - 1 - tap
                    dxbc = dxbc + dconv[ahead : ahead + seq, t] * pv[tap : tap + 1, t]
                dzx[:, INNER + k * TILE : INNER + (k + 1) * TILE] = dxbc.astype(BF16)
            if "all_o" in r:
                target = r["all_o"].at[:, width + INNER : width + INNER + XBC + LANES]
                outs.append(copies.start(dzx.at[:, INNER : INNER + XBC + LANES], target))
            else:
                outs.append(copies.start(dzx.at[:, INNER : INNER + XBC + LANES], r["dside_o"]))
            dh = r["dh_v"]
            for waits in wait_in:
                ready(waits)
            for k in range(width // TILE):
                t = cols(k)
                dh[:, t] = mm(dzx[:, 0 : INNER + XBC], win[t, :], (1, 1)) + mm(draw_low, wdt[t, :], (1, 1))
            product = dh[...] * gain
            pulled = jnp.mean(product * x, axis=-1, keepdims=True) * scale * scale
            dx = g + scale * (product - x * pulled)
            small[6:7, 0:width] = jnp.sum(dh[...] * x * scale, axis=0, keepdims=True)
            dh[...] = dx
            r["dxb_v"][...] = dx.astype(BF16)
            if "dxb_o" in r:
                save("dxb_o", r["dxb_v"])
            save("dx_o", dh)
            save("small_o", small)

        if mode in ("start", "fwd", "both"):
            forward()
        if mode == "out":
            ready(loads)
        if mode in ("out", "fwd", "both"):
            project()
        if mode in ("both", "bwd", "gated", "scan"):
            backward()
        finish_outs()

    pl.when(lax.axis_index("section") == cfg["section"])(body)


RESIDUALS = ("gate", "xbc", "y", "raw", "xs")
COST = dict(start=8000, out=2000, fwd=9000, both=18000, bwd=13000, gated=5000, scan=10000)
RESIDUALS_USED = dict(
    bwd=RESIDUALS, gated=("gate", "y"), scan=("raw", "xs", "dy", "y", "xbc", "small", "head"), out=("u",)
)


def layer_call(
    name,
    section,
    slot,
    block,
    mode,
    args,
    weights,
    residual=None,
    kept=None,
    save=False,
    one_array=False,
    ahead=(),
):
    win, wout, wdt, pv = weights
    kept = kept or {}
    n = args["pieces"]
    seq, width = args["tok"].shape[1], args["tok"].shape[2]
    rows = width // n + INNER // n
    proj = INNER + XBC
    shapes = dict(
        gate=((seq, INNER), F32),
        xbc=((seq, XBC), F32),
        y=((seq, INNER), F32),
        raw=((seq, LANES), F32),
        xs=((seq, XBC), BF16),
        out=((seq, width), BF16),
        u=((seq, INNER), BF16),
        dy=((seq, INNER), F32),
        all=((seq, width + proj + LANES), BF16),
        head=((seq, width + INNER), BF16),
        dside=((seq, XBC + LANES), BF16),
        dx=((seq, width), F32),
        dxb=((seq, width), BF16),
        small=((8, XBC), F32),
    )
    for k in range(min(n, 2)):
        shapes[f"hu{k}"] = ((rows * (2 if n > 1 else 1), 2 * seq), BF16)
    inputs = [("lengths", args["lengths"], pl.BlockSpec(memory_space=pltpu.SMEM))]
    inputs.append(("tok", args["tok"], FAR) if section == 0 else ("arr", args["arr"], ANY))
    if mode in ("both", "bwd", "gated", "scan"):
        inputs.append(("cot", args["cot"], FAR) if section == 1 else ("arrg", args["arrg"], ANY))
    if mode not in ("out", "gated"):
        inputs += [(f"win{k}", w, FAR) for k, w in enumerate(win)]
    if mode != "out":
        inputs += [("wdt", wdt, FAR), ("pv", pv, FAR)]
    if mode not in ("start", "scan"):
        inputs += [(f"wout{k}", w, FAR) for k, w in enumerate(wout)]
    inputs += [(f"{k}_i", residual[k], FAR) for k in RESIDUALS_USED.get(mode, ())]
    inputs += [(f"ahead{k}", value, FAR) for k, value in enumerate(ahead)]
    outputs = []
    if mode in ("start", "fwd", "both"):
        outputs += [f"hu{k}" for k in range(min(n, 2))]
        if save:
            outputs += list(RESIDUALS)
    if mode == "start":
        outputs.append("u")
    if mode in ("out", "fwd", "both"):
        outputs.append("out")
    if mode in ("both", "bwd"):
        outputs += ["all"] if one_array else ["head", "dside"]
        outputs += ["dx", "small"]
        if section == 1:
            outputs.append("dxb")
    if mode == "gated":
        outputs += ["head", "dy", "small"]
    if mode == "scan":
        outputs += ["dside", "dx", "small"]
    aliases = {}
    for place, key in enumerate(outputs):
        if key in kept:
            aliases[len(inputs)] = place
            inputs.append((f"{key}_k", kept[key], FAR))
    scratch = dict(
        x_v=((seq, width), BF16),
        g_v=((seq, width), BF16),
        dout_v=((seq, width), BF16),
        out_v=((seq, width), BF16),
        dxb_v=((seq, width), BF16),
        win_v=((width, proj), BF16),
        wout_v=((INNER, width), BF16),
        wdt_v=((width, LANES), BF16),
        pv_v=(pv.shape, F32),
        gate_v=((seq, INNER), F32),
        xbc_v=((seq + PAD, XBC), F32),
        y_v=((seq, INNER), F32),
        raw_v=((seq, LANES), F32),
        xs_v=((seq, XBC), BF16),
        ht_v=((width, seq), BF16),
        u_v=((seq, INNER), BF16),
        ut_v=((INNER, seq), BF16),
        a_v=((seq, INNER), F32),
        dact_v=((seq, XBC), F32),
        dconv_v=((seq + PAD, XBC), F32),
        dzx_v=((seq, proj + LANES), BF16),
        dh_v=((seq, width), F32),
        small_v=((8, XBC), F32),
    )
    names = [k for k, _, _ in inputs] + [f"{k}_o" for k in outputs] + list(scratch) + ["sems"]
    cfg = dict(
        names=names, pieces=n, section=section, slot=slot, block=block, mode=mode, seq=seq, width=width
    )
    results = pl.pallas_call(
        functools.partial(layer_kernel, cfg),
        out_shape=[jax.ShapeDtypeStruct(*shapes[k]) for k in outputs],
        in_specs=[spec for _, _, spec in inputs],
        out_specs=[FAR for _ in outputs],
        scratch_shapes=[pltpu.VMEM(*v) for v in scratch.values()]
        + [pltpu.SemaphoreType.DMA((96,))],
        input_output_aliases=aliases,
        cost_estimate=pl.CostEstimate(flops=COST[mode] * 10**6, bytes_accessed=10**6, transcendentals=0),
        compiler_params=pltpu.CompilerParams(vmem_limit_bytes=VMEM_LIMIT),
        name=name,
    )(*[value for _, value, _ in inputs])
    return dict(zip(outputs, results))


def product_kernel(rows, places, parts, count, extra, *refs):
    lefts, first, second = refs[:count], refs[count : 2 * count], refs[2 * count : 3 * count]
    smalls = refs[3 * count : 3 * count + extra]
    outs, (left_v, right_v, small_v, sems) = refs[-4 - len(parts) : -4], refs[-4:]
    seq = first[0].shape[0]
    copies = Copies(sems)
    waits = []
    for k in range(count):
        start = 2 * k * seq
        waits.append(copies.start(lefts[k].at[rows, :], left_v.at[:, start : start + 2 * seq]))
        for slot, side in enumerate((first[k], second[k])):
            at = start + slot * seq
            waits.append(copies.start(side.at[:, places[slot]], right_v.at[at : at + seq, :]))
    for k in range(extra):
        waits.append(copies.start(smalls[k], small_v.at[k]))
    for copy in waits:
        copy.wait()
    if extra:
        total = small_v[0]
        for k in range(1, extra):
            total = total + small_v[k]
        half = total.shape[1] // 2
        total = jnp.concatenate([total[:, :half], total[:, half:]], axis=0)
        for out in outs[-2:]:
            out[out.shape[0] - 16 :, 0:half] = total.astype(out.dtype)
    for out, (height, above, at, size) in zip(outs, parts):
        for k in range(0, size, TILE):
            end = min(k + TILE, size)
            value = mm(left_v[above : above + height, :], right_v[:, at + k : at + end])
            out[0:height, k:end] = value.astype(out.dtype)


def weight_product(name, lefts, rows, first, second, places, parts, ahead=(), smalls=()):
    count = len(lefts)
    depth = 2 * count * first[0].shape[0]
    tall, wide = rows.stop - rows.start, places[0].stop - places[0].start
    shapes = [(part[0], part[3]) for part in parts]
    if smalls:
        shapes[-2:] = [(height + 16, size) for height, size in shapes[-2:]]
    return pl.pallas_call(
        functools.partial(product_kernel, rows, places, parts, count, len(smalls)),
        out_shape=[jax.ShapeDtypeStruct(shape, BF16) for shape in shapes],
        in_specs=[FAR] * (3 * count + len(smalls) + len(ahead)),
        out_specs=[pl.BlockSpec(memory_space=pltpu.VMEM) for _ in shapes],
        scratch_shapes=[
            pltpu.VMEM((tall, depth), BF16),
            pltpu.VMEM((depth, wide), BF16),
            pltpu.VMEM((2, 8, XBC), F32),
            pltpu.SemaphoreType.DMA((3 * count + 2,)),
        ],
        cost_estimate=pl.CostEstimate(flops=10**6, bytes_accessed=10**6, transcendentals=0),
        compiler_params=pltpu.CompilerParams(vmem_limit_bytes=VMEM_LIMIT),
        name=name,
    )(*lefts, *first, *second, *smalls, *ahead)


def across(block, axis, way):
    size = lax.axis_size(axis)
    route = [(i, i + way) for i in range(size) if 0 <= i + way < size]
    return lax.ppermute(block, axis, route)


def swap(block, axis, bits):
    size = lax.axis_size(axis)
    return lax.ppermute(block, axis, [(i, i ^ bits) for i in range(size)])


def after(value, *others):
    return lax.optimization_barrier((value,) + others)[0]


def spread(own):
    far = swap(own, "fsdp", 2)
    return [own, swap(own, "fsdp", 1), far, swap(far, "fsdp", 1)]


def beside(own):
    return [own, swap(own, "fsdp", 1)]


def quarter(value, parts, number):
    rows = value.shape[0] // parts
    return lax.dynamic_slice_in_dim(value, number * rows, rows, axis=0)


def in_order(pieces, me):
    odd, high = (me & 1) == 1, (me & 2) == 2
    a = jnp.where(odd, pieces[1], pieces[0])
    b = jnp.where(odd, pieces[0], pieces[1])
    c = jnp.where(odd, pieces[3], pieces[2])
    d = jnp.where(odd, pieces[2], pieces[3])
    low = [jnp.where(high, c, a), jnp.where(high, d, b)]
    return jnp.stack(low + [jnp.where(high, a, c), jnp.where(high, b, d)])


def group_sums(own_parts, far_parts, place):
    middle = (place == 1) | (place == 2)
    count = len(own_parts)
    arrived, halves, totals, outwards = [], [], [], []

    def done(values, k):
        return [values[k]] if 0 <= k < len(values) else []

    for step in range(count + 2):
        if step < count:
            far = after(far_parts[step], *done(arrived, step - 2), *done(halves, step - 3))
            arrived.append(swap(far, "fsdp", 2))
        k = step - 1
        if 0 <= k < count:
            own = (own_parts[k].astype(F32) + arrived[k].astype(F32)).astype(BF16)
            own = after(own, *done(halves, k - 2))
            inward = lax.ppermute(own, "dp", [(0, 1), (3, 2)])
            inward = after(inward, *done(arrived, k + 1), *done(totals, k - 2))
            halves.append((own.astype(F32) + inward.astype(F32)).astype(BF16))
        k = step - 2
        if 0 <= k < count:
            other = lax.ppermute(halves[k], "dp", [(1, 2), (2, 1)])
            other = after(other, *done(halves, k + 1), *done(outwards, k - 2))
            totals.append((halves[k].astype(F32) + other.astype(F32)).astype(BF16))
            ready = after(totals[k], *done(totals, k - 1))
            outwards.append(lax.ppermute(ready, "dp", [(1, 0), (2, 3)]))
    return [jnp.where(middle, t, o).astype(F32) for t, o in zip(totals, outwards)]


def on_device(
    tokens,
    cotangent,
    lengths,
    norm_gain,
    in_weight,
    dt_weight,
    conv_weight,
    conv_bias,
    dt_bias,
    a_log,
    skip,
    gated_gain,
    out_weight,
):
    n = lax.axis_size("fsdp")
    square = n == 4 and lax.axis_size("dp") == 4
    section = lax.axis_index("section")
    me = lax.axis_index("fsdp")
    seq, width = tokens.shape[1], tokens.shape[2]
    proj = INNER + XBC
    if square:
        in_pair = lax.axis_index("dp") & 1
        fetched = [quarter(in_weight[0], 4, 2 * in_pair + k) for k in range(2)]
        over = [swap(fetched[0], "fsdp", 2)]
        norm_gain = after(norm_gain, over[0], fetched[1])
        over.append(swap(fetched[1], "fsdp", 2))
    smalls = (norm_gain, conv_weight, conv_bias, dt_bias, a_log, skip, gated_gain, dt_weight)
    packed = jnp.concatenate([s[0].reshape(-1) for s in smalls])
    if square:
        win = [in_weight[0], swap(in_weight[0], "fsdp", 1)]
        past = [swap(part, "dp", 1) for part in over]
        win += [part for pair in zip(over, past) for part in pair]
        win += [swap(part, "fsdp", 1) for part in win[2:]]
        lengths, packed = lax.optimization_barrier((lengths.reshape(-1), packed))
        over_out = swap(quarter(after(out_weight[0], past[0], over[1]), 2, in_pair), "fsdp", 2)
        far_out = [over_out, swap(over_out, "dp", 1)]
        packed = in_order(spread(after(packed, past[0])), me)
    else:
        win = [lax.all_gather(in_weight[0], "fsdp", axis=0, tiled=True)]
        wout = [lax.all_gather(out_weight[0], "fsdp", axis=0, tiled=True)]
        packed = lax.all_gather(packed, "fsdp", axis=0)
        lengths = lengths.reshape(-1)
    parts, place = [], 0
    for s in smalls:
        size = s.size
        parts.append(packed[:, place : place + size].reshape((n,) + s.shape[1:]))
        place += size

    def row(v, size=XBC):
        v = v.reshape(1, -1).astype(F32)
        return jnp.pad(v, ((0, 0), (0, size - v.shape[1])))

    conv_w = parts[1].transpose(1, 0, 2).reshape(CONV, XBC).astype(F32)
    sevens = jnp.concatenate([row(parts[3], LANES), row(parts[4], LANES), row(parts[5], LANES)], axis=1)
    pv = jnp.concatenate(
        [
            conv_w,
            row(parts[2]),
            row(parts[6]),
            row(parts[0]),
            row(sevens),
            row(jnp.repeat(parts[5].reshape(-1), HEAD_DIM)),
            jnp.zeros((7, XBC), F32),
        ]
    )
    wdt = jnp.pad(parts[7].reshape(width, HEADS), ((0, 0), (0, LANES - HEADS)))

    def keep(done, *keys):
        return {k: done[k] for k in done if k.startswith(keys)}

    at_zero = section == 0
    pieces = n if square else 1
    args = dict(tok=tokens, cot=cotangent, lengths=lengths, pieces=pieces)
    fwd_p = layer_call("start_p", 0, 0, 0, "start", args, (win, [], wdt, pv), save=True)
    if square:
        wout = [out_weight[0], swap(out_weight[0], "fsdp", 1), *far_out]
        wout += [swap(after(part, fwd_p["u"]), "fsdp", 1) for part in far_out]
    weights = (win, wout, wdt, pv)
    fwd_p.update(layer_call("out_p", 0, 0, 0, "out", args, weights, fwd_p))
    args["arr"] = across(fwd_p["out"], "section", 1)
    fwd_q = layer_call("fwd_q", 0, 1, 1, "fwd", args, weights, kept=keep(fwd_p, "hu"), save=True)
    arr_p = across(fwd_q["out"], "section", 1)
    both_q = layer_call("both_q", 1, 1, 0, "both", args, weights, kept=keep(fwd_q, "hu"))
    args["arrg"] = across(both_q["dxb"], "section", -1)
    args["arr"] = arr_p
    both_p = layer_call("both_p", 1, 0, 1, "both", args, weights, kept=keep(both_q, "hu"), one_array=True)
    arrg_q = across(both_p["dxb"], "section", -1)
    bwd_p = layer_call(
        "bwd_p", 0, 0, 0, "bwd", args, weights, fwd_p, keep(both_p, "all", "dx", "small"),
        one_array=True,
    )
    args["arrg"] = arrg_q
    gated_q = layer_call(
        "gated_q", 0, 1, 1, "gated", args, weights, fwd_q, keep(both_q, "head"),
        ahead=[bwd_p["dx"]],
    )
    rows_in, rows_out = width // pieces, INNER // pieces
    height = rows_in + rows_out
    hu, all_p, head_q = [both_p["hu0"]], [bwd_p["all"]], [gated_q["head"]]
    bases = (0,)
    if square:
        hu, all_p, head_q = hu + [swap(both_p["hu1"], "fsdp", 1)], beside(all_p[0]), beside(head_q[0])
        bases = (0, height)

    def parts_of(*parts):
        return tuple((size, base + row, at, wide) for size, row, at, wide in parts for base in bases)

    places = (slice(0, width + INNER),) * 2
    head_parts = (
        (rows_out // 2, rows_in, 0, width),
        (rows_out // 2, rows_in + rows_out // 2, 0, width),
        (rows_in, 0, width, INNER // 2),
        (rows_in, 0, width + INNER // 2, INNER // 2),
    )
    if not square:
        head_parts = ((rows_out, rows_in, 0, width), *head_parts[2:])
    parts = parts_of(*head_parts)
    grads = weight_product("grad_head", hu, slice(0, height * len(bases)), all_p, head_q, places, parts)
    scan_q = layer_call(
        "scan_q", 0, 1, 1, "scan", args, weights, {**fwd_q, **gated_q},
        keep(both_q, "dside", "dx", "small"), ahead=grads[:1],
    )
    small = bwd_p["small"] + scan_q["small"]
    side_q, smalls, ahead = [scan_q["dside"]], [], ()
    if square:
        side_q, smalls = beside(side_q[0]), beside(small)
    places = (slice(width + INNER, width + proj + LANES), slice(0, XBC + LANES))
    parts = parts_of((rows_in, 0, 0, CUT), (rows_in, 0, CUT, XBC + LANES - CUT))
    grads += weight_product(
        "grad_side", hu, slice(0, height * len(bases)), all_p, side_q, places, parts, (), smalls
    )

    def by_block(p, q):
        return jnp.stack([jnp.where(at_zero, p, q), jnp.where(at_zero, q, p)])

    outputs = by_block(
        jnp.where(at_zero, fwd_p["out"], both_p["out"]), jnp.where(at_zero, fwd_q["out"], both_q["out"])
    )
    input_grads = by_block(bwd_p["dx"], scan_q["dx"])
    if square:
        line = lax.axis_index("dp")
        grads = group_sums(grads[0::2], grads[1::2], line)
        small = grads[-1][rows_in:, : XBC // 2]
        small = jnp.concatenate([small[:8], small[8:]], axis=1)
    else:
        grads = [lax.psum_scatter(g, "fsdp", scatter_dimension=0, tiled=True) for g in grads]
        grads = [g.astype(F32) for g in lax.psum(grads, "dp")]
        small = lax.psum(small, ("dp", "fsdp"))
    def own(v):
        size = v.shape[-1] // n
        return lax.dynamic_slice_in_dim(v, me * size, size, axis=v.ndim - 1)

    owned = (
        own(small[6:7, :width]),
        own(small[None, 0:CONV]),
        own(small[4:5]),
        own(small[7:8, 0:HEADS]),
        own(small[7:8, LANES : LANES + HEADS]),
        own(small[7:8, 2 * LANES : 2 * LANES + HEADS]),
        own(small[5:6, :INNER]),
    )
    *grad_out, gate_low, gate_high, grad_near, grad_rest = grads
    rows_own = width // n

    grad_near = after(grad_near, *owned)
    return (
        outputs[None],
        input_grads[None],
        owned[0],
        jnp.concatenate([gate_low, gate_high, grad_near[:rows_own], grad_rest[:rows_own, : XBC - CUT]], axis=1)[None],
        grad_rest[None, :rows_own, XBC - CUT : XBC - CUT + HEADS],
        owned[1],
        owned[2],
        owned[3],
        owned[4],
        owned[5],
        owned[6],
        jnp.concatenate(grad_out)[None],
    )


def solution(mesh):
    in_specs = (
        P(None, ("dp", "fsdp"), None),
        P(None, ("dp", "fsdp"), None),
        P(None, ("dp", "fsdp")),
        P("section", "fsdp"),
        P("section", "fsdp", None),
        P("section", "fsdp", None),
        P("section", None, "fsdp"),
        P("section", "fsdp"),
        P("section", "fsdp"),
        P("section", "fsdp"),
        P("section", "fsdp"),
        P("section", "fsdp"),
        P("section", "fsdp", None),
    )
    out_specs = (
        P("section", None, ("dp", "fsdp"), None),
        P("section", None, ("dp", "fsdp"), None),
        P("section", "fsdp"),
        P("section", "fsdp", None),
        P("section", "fsdp", None),
        P("section", None, "fsdp"),
        P("section", "fsdp"),
        P("section", "fsdp"),
        P("section", "fsdp"),
        P("section", "fsdp"),
        P("section", "fsdp"),
        P("section", "fsdp", None),
    )
    return jax.shard_map(
        on_device, mesh=mesh, in_specs=in_specs, out_specs=out_specs, check_vma=False
    )
```
